32 devices in a mesh: group: 2 (over y), seq: 8 (over z, x), exp: 2 (over core).
Axes of the slice: x: 2, y: 2, z: 4, core: 2. Of those that a mesh axis runs over, the one named last changes fastest.
Arguments:
- tokens: bfloat16 [4096, 2048], P(('group', 'seq'), 'exp'), parts along dimension 0, may hold values from -20 to 20
- upstream: bfloat16 [4096, 2048], P(('group', 'seq'), 'exp'), parts along dimension 0, may hold values from -6 to 6
- slot_params: bfloat16 [64, 2048], P(('group', 'seq'), 'exp'), parts along dimension 0, may hold values from -3 to 3
- slot_outputs: bfloat16 [64, 2048], P(('group', 'seq', 'exp')), parts along dimension 0, may hold values from -6 to 6
- slot_input_grads: bfloat16 [64, 2048], P(('group', 'seq', 'exp')), parts along dimension 0, may hold values from -384 to 384
Outputs:
- token_grads: bfloat16 [4096, 2048], P(('group', 'seq'), 'exp'), parts along dimension 0
- param_grads: float32 [64, 2048], P(('group', 'seq'), 'exp'), parts along dimension 0
- slot_output_grads: float32 [64, 2048], P(('group', 'seq', 'exp')), parts along dimension 0
The draws below stay inside these ranges and needn't reach their ends.
There are 2 independent parts, one for each index of `group`. The reference program is written for one: setup_inputs(seed, part) draws one part's arguments, and reference() takes and returns one part's arrays. A program takes and returns all parts, laid end to end along the dimension named above; each array names one. Nothing has to cross between parts.
All inputs are finite; a program needn't handle non-finite values.
Results may differ from the reference program's by a relative error of at most 0.0052.
Values may be sent and summed in bfloat16 or wider, within the bound.
No kernel may reach another device: no remote copies, remote signals or barrier semaphores. Data moves between devices by JAX's collectives and lax.ppermute only.
A program may use at most 64 MiB of HBM per device.

```python
import jax
import jax.numpy as jnp

D = 2048
TOKENS = 2048
NS = 32


def draw_tokens(key, part):
    key = jax.random.fold_in(key, 11)
    first = jax.random.fold_in(key, 0)
    ramp = 0.5 * (1.0 + 2.0 * jnp.arange(TOKENS, dtype=jnp.float32) / TOKENS)
    base = jax.random.truncated_normal(first, -4.0, 4.0, (TOKENS, D), jnp.float32) * ramp[:, None]
    return base.astype(jnp.bfloat16)


def draw_slot_params(key, part):
    key = jax.random.fold_in(key, 12)
    first = jax.random.fold_in(key, 0)
    base = jax.random.truncated_normal(first, -4.0, 4.0, (NS, D), jnp.float32) * D ** (-0.5)
    return base.astype(jnp.bfloat16)


def block_levels(rng, dims, cuts, low, top_value):
    def one(position, parts):
        heights = jax.random.uniform(jax.random.fold_in(jax.random.fold_in(rng, 6), position), (parts,), jnp.float32, low / len(cuts), top_value / len(cuts))
        return jnp.repeat(jnp.exp(heights), dims[position] // parts).reshape((-1,) + (1,) * (len(dims) - position - 1))

    level = one(*cuts[0])
    for cut in cuts[1:]:
        level = level * one(*cut)
    return level


def normal_values(stream_key, dims, spread, reach, cuts=(), kind=jnp.bfloat16):
    values = jax.random.normal(stream_key, dims, jnp.float32) * spread
    if len(cuts) > 0:
        values = block_levels(stream_key, dims, cuts, -0.22, 0.18) * values
    return jnp.clip(values, min=-reach, max=reach).astype(kind)


def setup_inputs(seed: int = 0, part: int = 0) -> dict:
    key_list = jax.random.split(jax.random.key(seed), 6)
    part_keys = jax.random.split(jax.random.fold_in(key_list[5], part), 6)
    return {
        "tokens": draw_tokens(jax.random.fold_in(jax.random.fold_in(key_list[5], part), 71), part),
        "upstream": normal_values(part_keys[1], (TOKENS, D), 1.0, 6.0, ((0, 8), (1, 2))),
        "slot_params": draw_slot_params(jax.random.fold_in(jax.random.fold_in(key_list[5], part), 71), part),
        "slot_outputs": normal_values(part_keys[3], (NS, D), 1.0, 6.0, ((0, 16),)),
        "slot_input_grads": normal_values(part_keys[4], (NS, D), (TOKENS / NS), 384.0, ((0, 16),)),
    }


def reference(tokens, upstream, slot_params, slot_outputs, slot_input_grads):
    logits = jnp.dot(tokens, slot_params.T, preferred_element_type=jnp.float32)
    combine = jax.nn.softmax(logits, axis=1)
    dispatch = jax.nn.softmax(logits, axis=0)
    combine_b = combine.astype(jnp.bfloat16)
    dispatch_b = dispatch.astype(jnp.bfloat16)
    slot_output_grads = jnp.dot(combine_b.T, upstream, preferred_element_type=jnp.float32)
    d_comb = jnp.dot(upstream, slot_outputs.T, preferred_element_type=jnp.float32)
    d_disp = jnp.dot(tokens, slot_input_grads.T, preferred_element_type=jnp.float32)
    row_inner = jnp.sum(combine * d_comb, axis=1, keepdims=True)
    col_inner = jnp.sum(dispatch * d_disp, axis=0, keepdims=True)
    d_logit = combine * (d_comb - row_inner) + dispatch * (d_disp - col_inner)
    d_logit_b = d_logit.astype(jnp.bfloat16)
    token_grads = jnp.dot(dispatch_b, slot_input_grads, preferred_element_type=jnp.float32)
    token_grads = token_grads + jnp.dot(d_logit_b, slot_params, preferred_element_type=jnp.float32)
    param_grads = jnp.dot(d_logit_b.T, tokens, preferred_element_type=jnp.float32)
    return token_grads.astype(jnp.bfloat16), param_grads, slot_output_grads
```

```python
import functools

import jax
import jax.numpy as jnp
from jax import lax
from jax.experimental import pallas as pl
from jax.experimental.pallas import tpu as pltpu
from jax.sharding import PartitionSpec as P

F32 = jnp.float32
BF16 = jnp.bfloat16


def dot_nt(left, right):
    return lax.dot_general(left, right, (((1,), (1,)), ((), ())), preferred_element_type=F32)


def dot_tn(left, right):
    return lax.dot_general(left, right, (((0,), (0,)), ((), ())), preferred_element_type=F32)


def call(kernel, outs, name, seq, scratch=()):
    return pl.pallas_call(
        kernel,
        out_shape=outs,
        scratch_shapes=list(scratch),
        compiler_params=pltpu.CompilerParams(vmem_limit_bytes=(16 if seq <= 16 else 48) << 20),
        name=name,
    )


def split16(value):
    high = value.astype(BF16).astype(F32)
    return high, (value - high).astype(BF16).astype(F32)


def pack_kernel(params_ref, outs_ref, grads_ref, chunks_ref):
    half = params_ref.shape[1]
    quarter = half // 2
    params = params_ref[...].astype(F32)
    outs = outs_ref[...].astype(F32)
    grads = grads_ref[...].astype(F32)
    for core in range(2):
        span = slice(core * half, (core + 1) * half)
        rows = jnp.concatenate([params, outs[:, span], grads[:, span]], axis=0)
        chunk = jnp.concatenate([rows[:, :quarter], rows[:, quarter:]], axis=0).astype(BF16)
        for dest in range(chunks_ref.shape[0] // 2):
            chunks_ref[2 * dest + core] = chunk


def partial_kernel(slots_ref, tokens_ref, upstream_ref, part_ref):
    side = lax.axis_index("exp")
    devices, _, quarter = slots_ref.shape
    n_slots = part_ref.shape[0] // 3
    rows = slots_ref[...].reshape(devices * 16, quarter)

    def halves(right_ref):
        first = dot_nt(rows, right_ref[:, :quarter]).reshape(devices, 16, -1)
        second = dot_nt(rows, right_ref[:, quarter:]).reshape(devices, 16, -1)
        return first[:, :8] + second[:, 8:]

    by_tokens = halves(tokens_ref)
    by_upstream = halves(upstream_ref)
    for chip in range(devices // 2):
        a, b = 2 * chip, 2 * chip + 1
        own = jnp.where(side == 0, by_tokens[a], by_tokens[b])
        base = 4 * chip
        part_ref[base : base + 4, :] = own[0:4]
        for device, at in ((a, base), (b, base + 2)):
            part_ref[n_slots + at : n_slots + at + 2, :] = by_upstream[device][4:6]
            part_ref[2 * n_slots + at : 2 * n_slots + at + 2, :] = by_tokens[device][6:8]


def local_kernel(
    mine_ref, other_ref, tokens_ref, upstream_ref, send_ref, col_ref, row_ref, disp_ref, up_ref, tok_ref
):
    n_slots = col_ref.shape[0]
    seq, _, width = send_ref.shape
    half = tokens_ref.shape[1]
    extra = width - half
    groups = n_slots // 16 + 1
    both = mine_ref[...] + other_ref[...]
    logits, d_comb, d_disp = both[:n_slots], both[n_slots : 2 * n_slots], both[2 * n_slots :]
    row_exp = jnp.exp(logits - jnp.max(logits, axis=0, keepdims=True))
    combine = row_exp / jnp.sum(row_exp, axis=0, keepdims=True)
    row_part = combine * (d_comb - jnp.sum(combine * d_comb, axis=0, keepdims=True))
    top_high, top_low = split16(jnp.max(logits, axis=1, keepdims=True))
    col_exp = jnp.exp(logits - (top_high + top_low))
    sum_high, sum_low = split16(jnp.sum(col_exp, axis=1, keepdims=True))
    inner_high, inner_low = split16(jnp.sum(col_exp * d_disp, axis=1, keepdims=True))
    centre = (inner_high + inner_low) / (sum_high + sum_low)
    col_part = col_exp * (d_disp - centre)
    col_ref[...] = col_exp
    row_ref[...] = row_part
    disp_ref[...] = d_disp

    up_ref[...] = jnp.zeros_like(up_ref)
    tok_ref[...] = jnp.zeros_like(tok_ref)
    for chip in range(seq):
        span = slice(4 * chip, 4 * chip + 4)
        base = 16 * chip
        up_ref[base : base + 4, :] = combine[span]
        tok_ref[base + 4 : base + 8, :] = row_part[span]
        tok_ref[base + 8 : base + 12, :] = col_part[span]
        tok_ref[base + 12 : base + 16, :] = col_exp[span]
    sums = jnp.dot(up_ref[...].astype(BF16), upstream_ref[...], preferred_element_type=F32)
    sums = sums + jnp.dot(tok_ref[...].astype(BF16), tokens_ref[...], preferred_element_type=F32)
    send_ref[:, :, :half] = sums.astype(BF16).reshape(seq, 16, half)

    lane = lax.broadcasted_iota(jnp.int32, (n_slots, extra), 1)
    stats = jnp.zeros((n_slots, extra), F32)
    for j, stat in enumerate((top_high, top_low, sum_high, sum_low, inner_high, inner_low)):
        stats = jnp.where(lane == j * groups, stat, stats)
    every = jnp.zeros((16, extra), F32)
    for group in range(groups - 1):
        every = every + pltpu.roll(stats[16 * group : 16 * group + 16], group + 1, 1)
    for chip in range(seq):
        own = stats[4 * chip : 4 * chip + 4]
        block = every + jnp.concatenate([own, own, own, own], axis=0)
        send_ref[chip, :, half:] = block.astype(BF16)


def column_stats(stats, groups):
    extra = stats.shape[-1]
    axis = stats.ndim - 1
    pair = stats + pltpu.roll(stats, extra - groups, axis)
    return pair, pltpu.roll(pair, extra - 2 * groups, axis), pltpu.roll(pair, extra - 4 * groups, axis)


def merge_stats(got_ref, half, groups):
    seq = got_ref.shape[0]
    tops, totals, inners = [], [], []
    for chip in range(seq):
        top, total, inner = column_stats(got_ref[chip, :, half:].astype(F32), groups)
        tops.append(top)
        totals.append(total)
        inners.append(inner)
    high = functools.reduce(jnp.maximum, tops)
    scales = [jnp.exp(top - high) for top in tops]
    total = sum(scale * value for scale, value in zip(scales, totals))
    inner = sum(scale * value for scale, value in zip(scales, inners))
    weights = [scale / total for scale in scales]
    centres = [value / whole for value, whole in zip(inners, totals)]
    return high, total, inner / total, weights, centres


def sums_kernel(got_ref, params_ref, keep_ref, give_ref, *, groups):
    side = lax.axis_index("exp")
    half = params_ref.shape[1]
    _, _, centre, weights, centres = merge_stats(got_ref, half, groups)
    row = lax.broadcasted_iota(jnp.int32, centre.shape, 0)
    acc = jnp.zeros((16, half), F32)
    for chip, (weight, own) in enumerate(zip(weights, centres)):
        factor = jnp.where(row < 8, 1.0, jnp.where(row < 12, weight, weight * (own - centre)))
        acc = acc + factor[:, 0:1] * got_ref[chip, :, :half].astype(F32)
    params_ref[...] = acc[4:8] + acc[8:12] + acc[12:16]
    keep_ref[...] = jnp.where(side == 0, acc[0:2], acc[2:4])
    give_ref[...] = jnp.where(side == 0, acc[2:4], acc[0:2])


def tokens_kernel(got_ref, slots_ref, col_ref, row_ref, disp_ref, out_ref, left_ref, *, groups):
    side = lax.axis_index("exp")
    me = lax.axis_index("seq")
    half = out_ref.shape[1]
    quarter = half // 2
    devices = slots_ref.shape[0]
    n_slots = col_ref.shape[0]
    high, total, centre, _, _ = merge_stats(got_ref, half, groups)
    mine = got_ref[pl.ds(me, 1), :, half:][0].astype(F32)
    top, _, _ = column_stats(mine, groups)
    weight = jnp.exp(top - high) / total
    left_ref[...] = jnp.zeros_like(left_ref)
    for group in range(n_slots // 16):
        span = slice(16 * group, 16 * group + 16)
        dispatch = col_ref[span] * weight[:, group + 1 : group + 2]
        d_logit = row_ref[span] + dispatch * (disp_ref[span] - centre[:, group + 1 : group + 2])
        for j in range(4):
            chip = 4 * group + j
            ours = d_logit[4 * j : 4 * j + 4]
            left_ref[2 * chip, 0:4] = jnp.where(side == 0, ours, 0.0)
            left_ref[2 * chip + 1, 0:4] = jnp.where(side == 1, ours, 0.0)
            left_ref[2 * chip, 6:8] = dispatch[4 * j : 4 * j + 2]
            left_ref[2 * chip + 1, 6:8] = dispatch[4 * j + 2 : 4 * j + 4]
    left = left_ref[...]
    zero = jnp.zeros_like(left)
    right = slots_ref[...].reshape(devices * 16, quarter)
    for part, order in ((0, (left, zero)), (1, (zero, left))):
        rows = jnp.concatenate(order, axis=1).reshape(devices * 16, -1).astype(BF16)
        out_ref[:, part * quarter : (part + 1) * quarter] = dot_tn(rows, right).astype(out_ref.dtype)


def shards(seq, tokens, upstream, slot_params, slot_outputs, slot_input_grads):
    patches, half = tokens.shape
    n_slots = slot_params.shape[0] * seq
    groups = n_slots // 16 + 1
    extra = -(-6 * groups // 128) * 128
    sds = jax.ShapeDtypeStruct

    chunks = call(pack_kernel, sds((2 * seq, 16, half // 2), BF16), "pack", seq)(
        slot_params, slot_outputs, slot_input_grads
    )
    slots = lax.all_to_all(chunks, ("seq", "exp"), split_axis=0, concat_axis=0, tiled=True)
    part = call(partial_kernel, sds((3 * n_slots, patches), F32), "partial", seq)(slots, tokens, upstream)
    other = lax.ppermute(part, "exp", [(0, 1), (1, 0)])
    by_slot = sds((n_slots, patches), F32)
    send, col, row, disp = call(
        local_kernel,
        (sds((seq, 16, half + extra), BF16), by_slot, by_slot, by_slot),
        "local",
        seq,
        [pltpu.VMEM((16 * seq, patches), F32), pltpu.VMEM((16 * seq, patches), F32)],
    )(part, other, tokens, upstream)
    got = lax.all_to_all(send, "seq", split_axis=0, concat_axis=0, tiled=True)
    pair = sds((2, half), F32)
    param_grads, keep, give = call(
        functools.partial(sums_kernel, groups=groups), (sds((4, half), F32), pair, pair), "sums", seq
    )(got)
    taken = lax.ppermute(give, "exp", [(0, 1), (1, 0)])
    token_grads = call(
        functools.partial(tokens_kernel, groups=groups),
        sds((patches, half), BF16),
        "token_grads",
        seq,
        [pltpu.VMEM((2 * seq, 8, patches), F32)],
    )(got, slots, col, row, disp)
    side = lax.axis_index("exp")
    slot_output_grads = jnp.where(
        side == 0, jnp.concatenate([keep, taken], axis=1), jnp.concatenate([taken, keep], axis=1)
    )
    return token_grads, param_grads, slot_output_grads


def solution(mesh):
    in_specs = (
        P(("group", "seq"), "exp"),
        P(("group", "seq"), "exp"),
        P(("group", "seq"), "exp"),
        P(("group", "seq", "exp"), None),
        P(("group", "seq", "exp"), None),
    )
    out_specs = (
        P(("group", "seq"), "exp"),
        P(("group", "seq"), "exp"),
        P(("group", "seq", "exp"), None),
    )
    return jax.shard_map(
        functools.partial(shards, mesh.shape["seq"]),
        mesh=mesh,
        in_specs=in_specs,
        out_specs=out_specs,
        check_vma=False,
    )
```

```python
import functools

import jax
import jax.numpy as jnp
from jax import lax
from jax.experimental import pallas as pl
from jax.experimental.pallas import tpu as pltpu
from jax.sharding import PartitionSpec as P

F32 = jnp.float32
BF16 = jnp.bfloat16


def dot_nt(left, right):
    return lax.dot_general(left, right, (((1,), (1,)), ((), ())), preferred_element_type=F32)


def dot_tn(left, right):
    return lax.dot_general(left, right, (((0,), (0,)), ((), ())), preferred_element_type=F32)


def call(kernel, outs, name, seq, scratch=(), **specs):
    return pl.pallas_call(
        kernel,
        out_shape=outs,
        scratch_shapes=list(scratch),
        compiler_params=pltpu.CompilerParams(vmem_limit_bytes=(16 if seq <= 16 else 48) << 20),
        name=name,
        **specs,
    )


def split16(value):
    high = value.astype(BF16).astype(F32)
    return high, (value - high).astype(BF16).astype(F32)


def fetch_kernel(
    params_ref, outs_ref, grads_ref, upstream_ref, mine_ref, give_ref, held_ref, params, outs, grads, sems
):
    side = lax.axis_index("exp")
    half = params_ref.shape[1]
    sources, targets = (params_ref, outs_ref, grads_ref, upstream_ref), (params, outs, grads, held_ref)
    copies = [pltpu.make_async_copy(*pair, sems.at[i]) for i, pair in enumerate(zip(sources, targets))]
    for copy in copies:
        copy.start()
    for copy in copies[:3]:
        copy.wait()
    both = jnp.concatenate([outs[...].astype(F32), grads[...].astype(F32)], axis=0)
    first, second = both[:, :half], both[:, half:]
    mine_ref[0:4, :] = params[...].astype(F32)
    mine_ref[4:8, :] = jnp.where(side == 0, first, second)
    give_ref[...] = jnp.where(side == 0, second, first).astype(BF16)
    copies[3].wait()


def pack_kernel(mine_ref, taken_ref, chunks_ref):
    side = lax.axis_index("exp")
    half = mine_ref.shape[1]
    mine = mine_ref[...]
    own, taken = mine[4:8], taken_ref[...].astype(F32)
    first, second = jnp.where(side == 0, own, taken), jnp.where(side == 0, taken, own)
    outs = jnp.concatenate([first[0:2], second[0:2]], axis=0)
    left = jnp.concatenate([mine[0:4], first[2:4], second[2:4]], axis=0).astype(BF16)
    right = jnp.concatenate([outs[:, : half // 2], outs[:, half // 2 :]], axis=0).astype(BF16)
    for dest in range(chunks_ref.shape[0]):
        chunks_ref[dest, :, :half] = left
        chunks_ref[dest, :, half:] = right


def partial_kernel(slots_ref, tokens_ref, upstream_ref, part_ref):
    seq, _, width = slots_ref.shape
    half = tokens_ref.shape[1]
    quarter = half // 2
    n_slots = 4 * seq
    by_tokens = dot_nt(slots_ref[:, :, :half].reshape(8 * seq, half), tokens_ref[...])
    outs = slots_ref[:, :, half:].reshape(8 * seq, quarter)
    first = dot_nt(outs, upstream_ref[:, :quarter])
    second = dot_nt(outs, upstream_ref[:, quarter:])
    for chip in range(seq):
        at = 4 * chip
        base = 8 * chip
        part_ref[at : at + 4, :] = by_tokens[base : base + 4]
        part_ref[n_slots + at : n_slots + at + 4, :] = first[base : base + 4] + second[base + 4 : base + 8]
        part_ref[2 * n_slots + at : 2 * n_slots + at + 4, :] = by_tokens[base + 4 : base + 8]


def local_kernel(
    mine_ref, other_ref, tokens_ref, upstream_ref, send_ref, col_ref, row_ref, disp_ref, one_ref, two_ref, three_ref
):
    n_slots = col_ref.shape[0]
    seq, _, width = send_ref.shape
    half = tokens_ref.shape[1]
    extra = width - 2 * half
    groups = n_slots // 8 + 1
    both = mine_ref[...] + other_ref[...]
    logits, d_comb, d_disp = both[:n_slots], both[n_slots : 2 * n_slots], both[2 * n_slots :]
    row_exp = jnp.exp(logits - jnp.max(logits, axis=0, keepdims=True))
    combine = row_exp / jnp.sum(row_exp, axis=0, keepdims=True)
    row_part = combine * (d_comb - jnp.sum(combine * d_comb, axis=0, keepdims=True))
    top_high, top_low = split16(jnp.max(logits, axis=1, keepdims=True))
    col_exp = jnp.exp(logits - (top_high + top_low))
    sum_high, sum_low = split16(jnp.sum(col_exp, axis=1, keepdims=True))
    inner_high, inner_low = split16(jnp.sum(col_exp * d_disp, axis=1, keepdims=True))
    centre = (inner_high + inner_low) / (sum_high + sum_low)
    col_part = col_exp * (d_disp - centre)
    col_ref[...] = col_exp
    row_ref[...] = row_part
    disp_ref[...] = d_disp

    zero = jnp.zeros((4, col_ref.shape[1]), F32)
    for chip in range(seq):
        span = slice(4 * chip, 4 * chip + 4)
        upper, lower = slice(8 * chip, 8 * chip + 4), slice(8 * chip + 4, 8 * chip + 8)
        one_ref[upper, :] = combine[span]
        one_ref[lower, :] = zero
        two_ref[upper, :] = zero
        two_ref[lower, :] = col_part[span]
        three_ref[upper, :] = row_part[span]
        three_ref[lower, :] = col_exp[span]
    left = jnp.dot(one_ref[...].astype(BF16), upstream_ref[...], preferred_element_type=F32)
    left = left + jnp.dot(two_ref[...].astype(BF16), tokens_ref[...], preferred_element_type=F32)
    right = jnp.dot(three_ref[...].astype(BF16), tokens_ref[...], preferred_element_type=F32)
    send_ref[:, :, :half] = left.astype(BF16).reshape(seq, 8, half)
    send_ref[:, :, half : 2 * half] = right.astype(BF16).reshape(seq, 8, half)

    lane = lax.broadcasted_iota(jnp.int32, (n_slots, extra), 1)
    stats = jnp.zeros((n_slots, extra), F32)
    for j, stat in enumerate((top_high, top_low, sum_high, sum_low, inner_high, inner_low)):
        stats = jnp.where(lane == j * groups, stat, stats)
    every = jnp.zeros((8, extra), F32)
    for group in range(groups - 1):
        every = every + pltpu.roll(stats[8 * group : 8 * group + 8], group + 1, 1)
    for chip in range(seq):
        own = stats[4 * chip : 4 * chip + 4]
        send_ref[chip, :, 2 * half :] = (every + jnp.concatenate([own, own], axis=0)).astype(BF16)


def outs_kernel(got_ref, keep_ref, give_ref):
    side = lax.axis_index("exp")
    half = keep_ref.shape[1]
    acc = got_ref[0, :, :half].astype(F32)
    for chip in range(1, got_ref.shape[0]):
        acc = acc + got_ref[chip, :, :half].astype(F32)
    keep_ref[...] = jnp.where(side == 0, acc[0:2], acc[2:4])
    give_ref[...] = jnp.where(side == 0, acc[2:4], acc[0:2])


def column_stats(stats, groups):
    extra = stats.shape[1]
    pair = stats + pltpu.roll(stats, extra - groups, 1)
    return pair, pltpu.roll(pair, extra - 2 * groups, 1), pltpu.roll(pair, extra - 4 * groups, 1)


def sums_kernel(got_ref, col_ref, row_ref, disp_ref, params_ref, left_ref, rows_ref):
    me = lax.axis_index("seq")
    half = params_ref.shape[1]
    seq = got_ref.shape[0]
    n_slots = col_ref.shape[0]
    groups = n_slots // 8 + 1
    blocks = [column_stats(got_ref[chip, :, 2 * half :].astype(F32), groups) for chip in range(seq)]
    high = functools.reduce(jnp.maximum, [top for top, _, _ in blocks])
    scales = [jnp.exp(top - high) for top, _, _ in blocks]
    total = sum(scale * value for scale, (_, value, _) in zip(scales, blocks))
    centre = sum(scale * value for scale, (_, _, value) in zip(scales, blocks)) / total
    upper = lax.broadcasted_iota(jnp.int32, centre.shape, 0) < 4
    acc = jnp.zeros((8, half), F32)
    for chip, (scale, (_, own_total, own_inner)) in enumerate(zip(scales, blocks)):
        weight = scale / total
        by_left = jnp.where(upper, 0.0, weight)
        by_right = jnp.where(upper, 1.0, weight * (own_inner / own_total - centre))
        acc = acc + by_left[:, 0:1] * got_ref[chip, :, :half].astype(F32)
        acc = acc + by_right[:, 0:1] * got_ref[chip, :, half : 2 * half].astype(F32)
    params_ref[...] = acc[0:4] + acc[4:8]

    top, _, _ = column_stats(got_ref[pl.ds(me, 1), :, 2 * half :][0].astype(F32), groups)
    weight = jnp.exp(top - high) / total
    for group in range(groups - 1):
        span = slice(8 * group, 8 * group + 8)
        dispatch = col_ref[span] * weight[:, group + 1 : group + 2]
        d_logit = row_ref[span] + dispatch * (disp_ref[span] - centre[:, group + 1 : group + 2])
        for j in range(2):
            at = 16 * group + 8 * j
            rows_ref[at : at + 4, :] = d_logit[4 * j : 4 * j + 4]
            rows_ref[at + 4 : at + 8, :] = dispatch[4 * j : 4 * j + 4]
    left_ref[...] = rows_ref[...].astype(BF16)


def tokens_kernel(left_ref, slots_ref, keep_ref, taken_ref, out_ref, sums_ref):
    side = lax.axis_index("exp")
    half = out_ref.shape[1]
    right = slots_ref[:, :, :half].reshape(left_ref.shape[0], half)
    out_ref[...] = dot_tn(left_ref[...], right).astype(out_ref.dtype)
    keep, taken = keep_ref[...], taken_ref[...]
    sums_ref[:, :half] = jnp.where(side == 0, keep, taken)
    sums_ref[:, half:] = jnp.where(side == 0, taken, keep)


def shards(seq, tokens, upstream, slot_params, slot_outputs, slot_input_grads):
    patches, half = tokens.shape
    n_slots = slot_params.shape[0] * seq
    extra = -(-6 * (n_slots // 8 + 1) // 128) * 128
    sds = jax.ShapeDtypeStruct
    cores = [(0, 1), (1, 0)]

    mine, give, upstream = call(
        fetch_kernel,
        (sds((8, half), F32), sds((4, half), BF16), pltpu.VMEM(upstream.shape, BF16)),
        "fetch",
        seq,
        [
            pltpu.VMEM(slot_params.shape, BF16),
            pltpu.VMEM(slot_outputs.shape, BF16),
            pltpu.VMEM(slot_input_grads.shape, BF16),
            pltpu.SemaphoreType.DMA((4,)),
        ],
        in_specs=[pl.BlockSpec(memory_space=pl.ANY)] * 4,
    )(*(pltpu.with_memory_space_constraint(x, pltpu.HBM) for x in (slot_params, slot_outputs, slot_input_grads, upstream)))
    taken = lax.ppermute(give, "exp", cores)
    chunks = call(pack_kernel, sds((seq, 8, half + half // 2), BF16), "pack", seq)(mine, taken)
    slots = lax.all_to_all(chunks, "seq", split_axis=0, concat_axis=0, tiled=True)
    part = call(partial_kernel, sds((3 * n_slots, patches), F32), "partial", seq)(slots, tokens, upstream)
    other = lax.ppermute(part, "exp", cores)
    by_slot = sds((n_slots, patches), F32)
    send, col, row, disp = call(
        local_kernel,
        (sds((seq, 8, 2 * half + extra), BF16), by_slot, by_slot, by_slot),
        "local",
        seq,
        [pltpu.VMEM((8 * seq, patches), F32)] * 3,
    )(part, other, tokens, upstream)
    got = lax.all_to_all(send, "seq", split_axis=0, concat_axis=0, tiled=True)
    pair = sds((2, half), F32)
    keep, give = call(outs_kernel, (pair, pair), "outs", seq)(got)
    taken = lax.ppermute(give, "exp", cores)
    param_grads, left = call(
        sums_kernel,
        (sds((4, half), F32), sds((8 * seq, patches), BF16)),
        "sums",
        seq,
        [pltpu.VMEM((8 * seq, patches), F32)],
    )(got, col, row, disp)
    token_grads, slot_output_grads = call(
        tokens_kernel, (sds((patches, half), BF16), sds((2, 2 * half), F32)), "token_grads", seq
    )(left, slots, keep, taken)
    return token_grads, param_grads, slot_output_grads


def solution(mesh):
    in_specs = (
        P(("group", "seq"), "exp"),
        P(("group", "seq"), "exp"),
        P(("group", "seq"), "exp"),
        P(("group", "seq", "exp"), None),
        P(("group", "seq", "exp"), None),
    )
    out_specs = (
        P(("group", "seq"), "exp"),
        P(("group", "seq"), "exp"),
        P(("group", "seq", "exp"), None),
    )
    return jax.shard_map(
        functools.partial(shards, mesh.shape["seq"]),
        mesh=mesh,
        in_specs=in_specs,
        out_specs=out_specs,
        check_vma=False,
    )
```

```python
import functools

import jax
import jax.numpy as jnp
from jax import lax
from jax.experimental import pallas as pl
from jax.experimental.pallas import tpu as pltpu
from jax.sharding import PartitionSpec as P

F32 = jnp.float32
BF16 = jnp.bfloat16


def dot_nt(left, right):
    return lax.dot_general(left, right, (((1,), (1,)), ((), ())), preferred_element_type=F32)


def dot_tn(left, right):
    return lax.dot_general(left, right, (((0,), (0,)), ((), ())), preferred_element_type=F32)


def call(kernel, outs, name, seq, scratch=(), **specs):
    return pl.pallas_call(
        kernel,
        out_shape=outs,
        scratch_shapes=list(scratch),
        compiler_params=pltpu.CompilerParams(vmem_limit_bytes=(16 if seq <= 16 else 48) << 20),
        name=name,
        **specs,
    )


def split16(value):
    high = value.astype(BF16).astype(F32)
    return high, (value - high).astype(BF16).astype(F32)


def fetch_kernel(params_ref, outs_ref, grads_ref, mine_ref, params, outs, grads, sems):
    side = lax.axis_index("exp")
    half = params_ref.shape[1]
    quarter = half // 2
    sources, targets = (params_ref, outs_ref, grads_ref), (params, outs, grads)
    copies = [pltpu.make_async_copy(*pair, sems.at[i]) for i, pair in enumerate(zip(sources, targets))]
    for copy in copies:
        copy.start()
    for copy in copies:
        copy.wait()
    slot_outputs, slot_grads = outs[...].astype(F32), grads[...].astype(F32)
    own = jnp.where(side == 0, slot_outputs[:, :half], slot_outputs[:, half:])
    far = jnp.where(side == 0, slot_outputs[:, half:], slot_outputs[:, :half])
    mine_ref[0:4, :half] = params[...].astype(F32)
    for core in range(2):
        mine_ref[4 + 2 * core : 6 + 2 * core, :half] = jnp.where(side == 0, slot_grads[:, :half], slot_grads[:, half:])
    for i, block in enumerate((own[:, :quarter], own[:, quarter:], far[:, :quarter], far[:, quarter:])):
        mine_ref[2 * i : 2 * i + 2, half:] = block


def pack_kernel(mine_ref, grads_ref, chunks_ref):
    side = lax.axis_index("exp")
    width = mine_ref.shape[1]
    half = 2 * width // 3
    grads = grads_ref[...].astype(F32)
    taken = jnp.where(side == 0, grads[:, :half], grads[:, half:])
    mine = mine_ref[...]
    first, second = jnp.where(side == 0, mine[4:6, :half], taken), jnp.where(side == 0, taken, mine[6:8, :half])
    left = jnp.concatenate([mine[0:4, :half], first, second], axis=0).astype(BF16)
    right = mine[:, half:].astype(BF16)
    for dest in range(chunks_ref.shape[0]):
        chunks_ref[dest, :, :half] = left
        chunks_ref[dest, :, half:] = right


def partial_kernel(slots_ref, tokens_ref, upstream_ref, far_ref, part_ref):
    side = lax.axis_index("exp")
    seq, _, width = slots_ref.shape
    half = tokens_ref.shape[1]
    quarter = half // 2
    n_slots = 4 * seq
    by_tokens = dot_nt(slots_ref[:, :, :half].reshape(8 * seq, half), tokens_ref[...])
    outs = slots_ref[:, :, half:].reshape(8 * seq, quarter)
    pieces = (upstream_ref[:, :quarter], upstream_ref[:, quarter:], far_ref[:, :quarter], far_ref[:, quarter:])
    by_quarter = [dot_nt(outs, piece) for piece in pieces]
    for chip in range(seq):
        at = 4 * chip
        base = 8 * chip
        d_comb = sum(block[base + 2 * i : base + 2 * i + 2] for i, block in enumerate(by_quarter))
        part_ref[at : at + 4, :] = by_tokens[base : base + 4]
        part_ref[n_slots + at : n_slots + at + 2, :] = jnp.where(side == 0, d_comb, 0.0)
        part_ref[n_slots + at + 2 : n_slots + at + 4, :] = jnp.where(side == 1, d_comb, 0.0)
        part_ref[2 * n_slots + at : 2 * n_slots + at + 4, :] = by_tokens[base + 4 : base + 8]


def local_kernel(
    mine_ref, other_ref, tokens_ref, upstream_ref, far_ref, send_ref, col_ref, row_ref, disp_ref, *rows
):
    own_ref, cross_ref, two_ref, three_ref = rows
    side = lax.axis_index("exp")
    n_slots = col_ref.shape[0]
    seq, _, width = send_ref.shape
    half = tokens_ref.shape[1]
    extra = width - 2 * half
    groups = n_slots // 8 + 1
    both = mine_ref[...] + other_ref[...]
    logits, d_comb, d_disp = both[:n_slots], both[n_slots : 2 * n_slots], both[2 * n_slots :]
    row_exp = jnp.exp(logits - jnp.max(logits, axis=0, keepdims=True))
    combine = row_exp / jnp.sum(row_exp, axis=0, keepdims=True)
    row_part = combine * (d_comb - jnp.sum(combine * d_comb, axis=0, keepdims=True))
    top_high, top_low = split16(jnp.max(logits, axis=1, keepdims=True))
    col_exp = jnp.exp(logits - (top_high + top_low))
    sum_high, sum_low = split16(jnp.sum(col_exp, axis=1, keepdims=True))
    inner_high, inner_low = split16(jnp.sum(col_exp * d_disp, axis=1, keepdims=True))
    centre = (inner_high + inner_low) / (sum_high + sum_low)
    col_part = col_exp * (d_disp - centre)
    col_ref[...] = col_exp
    row_ref[...] = row_part
    disp_ref[...] = d_disp

    zero = jnp.zeros((4, col_ref.shape[1]), F32)
    ours = lax.broadcasted_iota(jnp.int32, zero.shape, 0) // 2 == side
    for chip in range(seq):
        span = slice(4 * chip, 4 * chip + 4)
        upper, lower = slice(8 * chip, 8 * chip + 4), slice(8 * chip + 4, 8 * chip + 8)
        kept = jnp.where(ours, combine[span], 0.0)
        own_ref[upper, :] = kept
        own_ref[lower, :] = zero
        cross_ref[upper, :] = jnp.concatenate([kept[2:4], kept[0:2]], axis=0)
        cross_ref[lower, :] = zero
        two_ref[upper, :] = zero
        two_ref[lower, :] = col_part[span]
        three_ref[upper, :] = row_part[span]
        three_ref[lower, :] = col_exp[span]
    left = jnp.dot(own_ref[...].astype(BF16), upstream_ref[...], preferred_element_type=F32)
    left = left + jnp.dot(cross_ref[...].astype(BF16), far_ref[...], preferred_element_type=F32)
    left = left + jnp.dot(two_ref[...].astype(BF16), tokens_ref[...], preferred_element_type=F32)
    right = jnp.dot(three_ref[...].astype(BF16), tokens_ref[...], preferred_element_type=F32)
    send_ref[:, :, :half] = left.astype(BF16).reshape(seq, 8, half)
    send_ref[:, :, half : 2 * half] = right.astype(BF16).reshape(seq, 8, half)

    lane = lax.broadcasted_iota(jnp.int32, (n_slots, extra), 1)
    stats = jnp.zeros((n_slots, extra), F32)
    for j, stat in enumerate((top_high, top_low, sum_high, sum_low, inner_high, inner_low)):
        stats = jnp.where(lane == j * groups, stat, stats)
    every = jnp.zeros((8, extra), F32)
    for group in range(groups - 1):
        every = every + pltpu.roll(stats[8 * group : 8 * group + 8], group + 1, 1)
    for chip in range(seq):
        own = stats[4 * chip : 4 * chip + 4]
        send_ref[chip, :, 2 * half :] = (every + jnp.concatenate([own, own], axis=0)).astype(BF16)


def column_stats(stats, groups):
    extra = stats.shape[1]
    pair = stats + pltpu.roll(stats, extra - groups, 1)
    return pair, pltpu.roll(pair, extra - 2 * groups, 1), pltpu.roll(pair, extra - 4 * groups, 1)


def finish_kernel(
    got_ref, slots_ref, col_ref, row_ref, disp_ref, *outs_and_scratch
):
    params_out, tokens_out, sums_out, rows_ref, params_ref, tokens_ref, sums_ref, sems = outs_and_scratch
    me = lax.axis_index("seq")
    half = params_ref.shape[1]
    seq = got_ref.shape[0]
    n_slots = col_ref.shape[0]
    groups = n_slots // 8 + 1
    blocks = [column_stats(got_ref[chip, :, 2 * half :].astype(F32), groups) for chip in range(seq)]
    high = functools.reduce(jnp.maximum, [top for top, _, _ in blocks])
    scales = [jnp.exp(top - high) for top, _, _ in blocks]
    total = sum(scale * value for scale, (_, value, _) in zip(scales, blocks))
    centre = sum(scale * value for scale, (_, _, value) in zip(scales, blocks)) / total

    top, _, _ = column_stats(got_ref[pl.ds(me, 1), :, 2 * half :][0].astype(F32), groups)
    weight = jnp.exp(top - high) / total
    for group in range(groups - 1):
        span = slice(8 * group, 8 * group + 8)
        dispatch = col_ref[span] * weight[:, group + 1 : group + 2]
        d_logit = row_ref[span] + dispatch * (disp_ref[span] - centre[:, group + 1 : group + 2])
        for j in range(2):
            at = 16 * group + 8 * j
            rows_ref[at : at + 4, :] = d_logit[4 * j : 4 * j + 4]
            rows_ref[at + 4 : at + 8, :] = dispatch[4 * j : 4 * j + 4]
    right = slots_ref[:, :, :half].reshape(8 * seq, half)
    left = rows_ref[...].astype(BF16)
    patches = tokens_ref.shape[0] // 2
    copies = []
    for part in range(2):
        span = slice(part * patches, (part + 1) * patches)
        tokens_ref[span, :] = dot_tn(left[:, span], right).astype(BF16)
        copies.append(pltpu.make_async_copy(tokens_ref.at[span], tokens_out.at[span], sems.at[part]))
        copies[-1].start()

    upper = lax.broadcasted_iota(jnp.int32, centre.shape, 0) < 4
    left = right = jnp.zeros((8, half), F32)
    for chip, (scale, (_, own_total, own_inner)) in enumerate(zip(scales, blocks)):
        weight = scale / total
        by_left = jnp.where(upper, 1.0, weight)
        by_right = jnp.where(upper, 1.0, weight * (own_inner / own_total - centre))
        left = left + by_left[:, 0:1] * got_ref[chip, :, :half].astype(F32)
        right = right + by_right[:, 0:1] * got_ref[chip, :, half : 2 * half].astype(F32)
    sums_ref[:, :half] = left[0:2]
    sums_ref[:, half:] = left[2:4]
    params_ref[...] = left[4:8] + right[0:4] + right[4:8]
    for i, (source, target) in enumerate(((params_ref, params_out), (sums_ref, sums_out))):
        copies.append(pltpu.make_async_copy(source, target, sems.at[2 + i]))
        copies[-1].start()
    for copy in copies:
        copy.wait()


def shards(seq, tokens, upstream, slot_params, slot_outputs, slot_input_grads):
    patches, half = tokens.shape
    n_slots = slot_params.shape[0] * seq
    extra = -(-6 * (n_slots // 8 + 1) // 128) * 128
    sds = jax.ShapeDtypeStruct
    cores = [(0, 1), (1, 0)]

    grads_far = lax.ppermute(slot_input_grads, "exp", cores)
    far = lax.ppermute(upstream, "exp", cores)
    mine = call(
        fetch_kernel,
        sds((8, half + half // 2), F32),
        "fetch",
        seq,
        [
            pltpu.VMEM(slot_params.shape, BF16),
            pltpu.VMEM(slot_outputs.shape, BF16),
            pltpu.VMEM(slot_input_grads.shape, BF16),
            pltpu.SemaphoreType.DMA((3,)),
        ],
        in_specs=[pl.BlockSpec(memory_space=pl.ANY)] * 3,
        cost_estimate=pl.CostEstimate(flops=10000000000, bytes_accessed=10000000, transcendentals=0),
    )(*(pltpu.with_memory_space_constraint(x, pltpu.HBM) for x in (slot_params, slot_outputs, slot_input_grads)))
    chunks = call(pack_kernel, sds((seq, 8, half + half // 2), BF16), "pack", seq)(mine, grads_far)
    slots = lax.all_to_all(chunks, "seq", split_axis=0, concat_axis=0, tiled=True)
    part = call(partial_kernel, sds((3 * n_slots, patches), F32), "partial", seq)(slots, tokens, upstream, far)
    other = lax.ppermute(part, "exp", cores)
    by_slot = sds((n_slots, patches), F32)
    send, col, row, disp = call(
        local_kernel,
        (sds((seq, 8, 2 * half + extra), BF16), by_slot, by_slot, by_slot),
        "local",
        seq,
        [pltpu.VMEM((8 * seq, patches), F32)] * 4,
    )(part, other, tokens, upstream, far)
    got = lax.all_to_all(send, "seq", split_axis=0, concat_axis=0, tiled=True)
    param_grads, token_grads, slot_output_grads = call(
        finish_kernel,
        (sds((4, half), F32), sds((patches, half), BF16), sds((2, 2 * half), F32)),
        "finish",
        seq,
        [
            pltpu.VMEM((8 * seq, patches), F32),
            pltpu.VMEM((4, half), F32),
            pltpu.VMEM((patches, half), BF16),
            pltpu.VMEM((2, 2 * half), F32),
            pltpu.SemaphoreType.DMA((4,)),
        ],
        out_specs=[pl.BlockSpec(memory_space=pl.ANY)] * 3,
    )(got, slots, col, row, disp)
    return token_grads, param_grads, slot_output_grads


def solution(mesh):
    in_specs = (
        P(("group", "seq"), "exp"),
        P(("group", "seq"), "exp"),
        P(("group", "seq"), "exp"),
        P(("group", "seq", "exp"), None),
        P(("group", "seq", "exp"), None),
    )
    out_specs = (
        P(("group", "seq"), "exp"),
        P(("group", "seq"), "exp"),
        P(("group", "seq", "exp"), None),
    )
    return jax.shard_map(
        functools.partial(shards, mesh.shape["seq"]),
        mesh=mesh,
        in_specs=in_specs,
        out_specs=out_specs,
        check_vma=False,
    )
```

```python
import functools

import jax
import jax.numpy as jnp
from jax import lax
from jax.experimental import pallas as pl
from jax.experimental.pallas import tpu as pltpu
from jax.sharding import PartitionSpec as P

F32 = jnp.float32
BF16 = jnp.bfloat16
LONG = pl.CostEstimate(flops=10**10, bytes_accessed=10**7, transcendentals=0)


def dot_nt(left, right):
    return lax.dot_general(left, right, (((1,), (1,)), ((), ())), preferred_element_type=F32)


def dot_tn(left, right):
    return lax.dot_general(left, right, (((0,), (0,)), ((), ())), preferred_element_type=F32)


def call(kernel, outs, name, seq, scratch=(), **specs):
    return pl.pallas_call(
        kernel,
        out_shape=outs,
        scratch_shapes=list(scratch),
        compiler_params=pltpu.CompilerParams(vmem_limit_bytes=(16 if seq <= 16 else 48) << 20),
        name=name,
        **specs,
    )


def split16(value):
    high = value.astype(BF16).astype(F32)
    return high, (value - high).astype(BF16).astype(F32)


def seed_kernel(seed_ref):
    seed_ref[...] = jnp.zeros_like(seed_ref)


def pack_kernel(seed_ref, params_ref, outs_ref, grads_ref, chunks_ref):
    side = lax.axis_index("exp")
    half = params_ref.shape[1]
    quarter = half // 2

    def halves(ref):
        value = ref[...].astype(F32)
        first, second = value[:, :half], value[:, half:]
        return jnp.where(side == 0, first, second), jnp.where(side == 0, second, first)

    own, far = halves(outs_ref)
    pieces = (own[:, :quarter], own[:, quarter:], far[:, :quarter], far[:, quarter:])
    left = jnp.concatenate([params_ref[...].astype(F32), *halves(grads_ref)], axis=0).astype(BF16)
    right = jnp.concatenate(pieces, axis=0).astype(BF16)
    for dest in range(chunks_ref.shape[0]):
        chunks_ref[dest, :, :half] = left
        chunks_ref[dest, :, half:] = right


def products(slots_ref, tokens_ref, tokens_far_ref, upstream_ref, upstream_far_ref, side):
    seq, _, width = slots_ref.shape
    half = tokens_ref.shape[1]
    quarter = half // 2
    left = slots_ref[:, :, :half].reshape(8 * seq, half)
    right = slots_ref[:, :, half:].reshape(8 * seq, quarter)
    near, far = dot_nt(left, tokens_ref[...]), dot_nt(left, tokens_far_ref[...])
    by_quarter = [
        dot_nt(right, ref[:, i * quarter : (i + 1) * quarter])
        for ref in (upstream_ref, upstream_far_ref)
        for i in range(2)
    ]
    row = lax.broadcasted_iota(jnp.int32, (8, near.shape[1]), 0)
    ours = row // 2 % 2 == side
    blocks = []
    for chip in range(0, seq, 2):
        parts = []
        for at in (8 * chip, 8 * chip + 8):
            one, two, three, four = (block[at : at + 8] for block in by_quarter)
            comb = jnp.where(row < 4, jnp.where(row < 2, one, two), jnp.where(row < 6, three, four))
            disp = jnp.where(row < 4, 0.0, jnp.where(row < 6, near[at : at + 8], far[at : at + 8]))
            comb, disp = comb + pltpu.roll(comb, 4, 0), disp + pltpu.roll(disp, 4, 0)
            comb, disp = comb + pltpu.roll(comb, 2, 0), disp + pltpu.roll(disp, 2, 0)
            parts.append((near[at : at + 8], comb, disp))
        (even, even_comb, even_disp), (odd, odd_comb, odd_disp) = parts
        logits = jnp.where(row < 4, even, pltpu.roll(odd, 4, 0))
        comb = jnp.where(ours, jnp.where(row < 4, even_comb, odd_comb), 0.0)
        disp = jnp.where(ours, jnp.where(row < 4, even_disp, odd_disp), 0.0)
        blocks.append((logits, comb, disp))
    return [jnp.concatenate(parts, axis=0) for parts in zip(*blocks)]


def near_kernel(slots_ref, tokens_ref, tokens_far_ref, upstream_ref, upstream_far_ref, *part_refs):
    side = lax.axis_index("exp")
    parts = products(slots_ref, tokens_ref, tokens_far_ref, upstream_ref, upstream_far_ref, side)
    for ref, part in zip(part_refs, parts):
        ref[...] = part


def local_kernel(
    slots_ref, tokens_ref, tokens_far_ref, upstream_ref, upstream_far_ref, logit_ref, comb_ref, disp_ref, *outs
):
    send_ref, col_ref, row_ref, d_disp_ref, own_ref, cross_ref, tokens_rows_ref = outs
    side = lax.axis_index("exp")
    n_slots = col_ref.shape[0]
    seq, _, width = send_ref.shape
    half = tokens_ref.shape[1]
    extra = width - 2 * half
    groups = n_slots // 8 + 1
    parts = products(slots_ref, tokens_far_ref, tokens_ref, upstream_far_ref, upstream_ref, 1 - side)
    logits, d_comb, d_disp = (ref[...] + part for ref, part in zip((logit_ref, comb_ref, disp_ref), parts))
    row_exp = jnp.exp(logits - jnp.max(logits, axis=0, keepdims=True))
    combine = row_exp / jnp.sum(row_exp, axis=0, keepdims=True)
    row_part = combine * (d_comb - jnp.sum(combine * d_comb, axis=0, keepdims=True))
    top_high, top_low = split16(jnp.max(logits, axis=1, keepdims=True))
    col_exp = jnp.exp(logits - (top_high + top_low))
    sum_high, sum_low = split16(jnp.sum(col_exp, axis=1, keepdims=True))
    inner_high, inner_low = split16(jnp.sum(col_exp * d_disp, axis=1, keepdims=True))
    centre = (inner_high + inner_low) / (sum_high + sum_low)
    col_part = col_exp * (d_disp - centre)
    col_ref[...] = col_exp
    row_ref[...] = row_part
    d_disp_ref[...] = d_disp

    zero = jnp.zeros((4, col_ref.shape[1]), F32)
    ours = lax.broadcasted_iota(jnp.int32, zero.shape, 0) // 2 == side
    for chip in range(seq):
        span = slice(4 * chip, 4 * chip + 4)
        upper, lower = slice(8 * chip, 8 * chip + 4), slice(8 * chip + 4, 8 * chip + 8)
        kept = jnp.where(ours, combine[span], 0.0)
        own_ref[upper, :] = kept
        own_ref[lower, :] = zero
        cross_ref[upper, :] = jnp.concatenate([kept[2:4], kept[0:2]], axis=0)
        cross_ref[lower, :] = zero
        tokens_rows_ref[0, upper, :] = zero
        tokens_rows_ref[0, lower, :] = col_part[span]
        tokens_rows_ref[1, upper, :] = row_part[span]
        tokens_rows_ref[1, lower, :] = col_exp[span]
    left = jnp.dot(own_ref[...].astype(BF16), upstream_ref[...], preferred_element_type=F32)
    left = left + jnp.dot(cross_ref[...].astype(BF16), upstream_far_ref[...], preferred_element_type=F32)
    rows = tokens_rows_ref[...].reshape(16 * seq, -1).astype(BF16)
    by_tokens = jnp.dot(rows, tokens_ref[...], preferred_element_type=F32)
    left, right = left + by_tokens[: 8 * seq], by_tokens[8 * seq :]
    send_ref[:, :, :half] = left.astype(BF16).reshape(seq, 8, half)
    send_ref[:, :, half : 2 * half] = right.astype(BF16).reshape(seq, 8, half)

    lane = lax.broadcasted_iota(jnp.int32, (n_slots, extra), 1)
    stats = jnp.zeros((n_slots, extra), F32)
    for j, stat in enumerate((top_high, top_low, sum_high, sum_low, inner_high, inner_low)):
        stats = jnp.where(lane == j * groups, stat, stats)
    every = jnp.zeros((8, extra), F32)
    for group in range(groups - 1):
        every = every + pltpu.roll(stats[8 * group : 8 * group + 8], group + 1, 1)
    for chip in range(seq):
        own = stats[4 * chip : 4 * chip + 4]
        send_ref[chip, :, 2 * half :] = (every + jnp.concatenate([own, own], axis=0)).astype(BF16)


def column_stats(stats, groups):
    extra = stats.shape[1]
    pair = stats + pltpu.roll(stats, extra - groups, 1)
    return pair, pltpu.roll(pair, extra - 2 * groups, 1), pltpu.roll(pair, extra - 4 * groups, 1)


def finish_kernel(
    got_ref, slots_ref, other_ref, col_ref, row_ref, disp_ref, *outs_and_scratch
):
    params_out, tokens_out, sums_out, rows_ref, params_ref, tokens_ref, sums_ref, sems = outs_and_scratch
    me, side = lax.axis_index("seq"), lax.axis_index("exp")
    half = params_ref.shape[1]
    seq = got_ref.shape[0]
    n_slots = col_ref.shape[0]
    groups = n_slots // 8 + 1
    blocks = [column_stats(got_ref[chip, :, 2 * half :].astype(F32), groups) for chip in range(seq)]
    high = functools.reduce(jnp.maximum, [top for top, _, _ in blocks])
    scales = [jnp.exp(top - high) for top, _, _ in blocks]
    total = sum(scale * value for scale, (_, value, _) in zip(scales, blocks))
    centre = sum(scale * value for scale, (_, _, value) in zip(scales, blocks)) / total

    top, _, _ = column_stats(got_ref[pl.ds(me, 1), :, 2 * half :][0].astype(F32), groups)
    weight = jnp.exp(top - high) / total
    zero = jnp.zeros((6, col_ref.shape[1]), F32)
    for group in range(groups - 1):
        span = slice(8 * group, 8 * group + 8)
        dispatch = col_ref[span] * weight[:, group + 1 : group + 2]
        d_logit = row_ref[span] + dispatch * (disp_ref[span] - centre[:, group + 1 : group + 2])
        first = jnp.where(side == 0, dispatch, pltpu.roll(dispatch, 6, 0))
        second = jnp.where(side == 0, pltpu.roll(dispatch, 6, 0), dispatch)
        for j in range(2):
            span = slice(16 * group + 8 * j, 16 * group + 8 * j + 8)
            ours, theirs = first[4 * j : 4 * j + 2], second[4 * j : 4 * j + 2]
            rows_ref[0, span, :] = jnp.concatenate([d_logit[4 * j : 4 * j + 4], ours, zero[0:2]], axis=0)
            rows_ref[1, span, :] = jnp.concatenate([zero, theirs], axis=0)
    left = rows_ref[...].reshape(16 * seq, -1).astype(BF16)
    right = jnp.concatenate([ref[:, :, :half].reshape(8 * seq, half) for ref in (slots_ref, other_ref)], axis=0)
    patches = tokens_ref.shape[0] // 2
    copies = []
    for part in range(2):
        span = slice(part * patches, (part + 1) * patches)
        tokens_ref[span, :] = dot_tn(left[:, span], right).astype(BF16)
        copies.append(pltpu.make_async_copy(tokens_ref.at[span], tokens_out.at[span], sems.at[part]))
        copies[-1].start()

    upper = lax.broadcasted_iota(jnp.int32, centre.shape, 0) < 4
    left = right = jnp.zeros((8, half), F32)
    for chip, (scale, (_, own_total, own_inner)) in enumerate(zip(scales, blocks)):
        weight = scale / total
        by_left = jnp.where(upper, 1.0, weight)
        by_right = jnp.where(upper, 1.0, weight * (own_inner / own_total - centre))
        left = left + by_left[:, 0:1] * got_ref[chip, :, :half].astype(F32)
        right = right + by_right[:, 0:1] * got_ref[chip, :, half : 2 * half].astype(F32)
    sums_ref[:, :half] = left[0:2]
    sums_ref[:, half:] = left[2:4]
    params_ref[...] = left[4:8] + right[0:4] + right[4:8]
    for i, (source, target) in enumerate(((params_ref, params_out), (sums_ref, sums_out))):
        copies.append(pltpu.make_async_copy(source, target, sems.at[2 + i]))
        copies[-1].start()
    for copy in copies:
        copy.wait()


def shards(seq, tokens, upstream, slot_params, slot_outputs, slot_input_grads):
    patches, half = tokens.shape
    n_slots = slot_params.shape[0] * seq
    extra = -(-6 * (n_slots // 8 + 1) // 128) * 128
    sds = jax.ShapeDtypeStruct
    cores = [(0, 1), (1, 0)]

    tokens_far, far = (lax.ppermute(x, "exp", cores) for x in (tokens, upstream))
    seed = call(seed_kernel, sds((8, 128), F32), "seed", seq, cost_estimate=LONG)()
    chunks = call(pack_kernel, sds((seq, 8, half + half // 2), BF16), "pack", seq)(
        seed, slot_params, slot_outputs, slot_input_grads
    )
    slots = lax.all_to_all(chunks, "seq", split_axis=0, concat_axis=0, tiled=True)
    other = lax.ppermute(slots, "exp", cores)
    by_slot = sds((n_slots, patches), F32)
    near = call(near_kernel, (by_slot,) * 3, "near", seq, cost_estimate=LONG)(slots, tokens, tokens_far, upstream, far)
    send, col, row, disp = call(
        local_kernel,
        (sds((seq, 8, 2 * half + extra), BF16), by_slot, by_slot, by_slot),
        "local",
        seq,
        [pltpu.VMEM((8 * seq, patches), F32)] * 2 + [pltpu.VMEM((2, 8 * seq, patches), F32)],
    )(other, tokens, tokens_far, upstream, far, *near)
    got = lax.all_to_all(send, "seq", split_axis=0, concat_axis=0, tiled=True)
    param_grads, token_grads, slot_output_grads = call(
        finish_kernel,
        (sds((4, half), F32), sds((patches, half), BF16), sds((2, 2 * half), F32)),
        "finish",
        seq,
        [
            pltpu.VMEM((2, 8 * seq, patches), F32),
            pltpu.VMEM((4, half), F32),
            pltpu.VMEM((patches, half), BF16),
            pltpu.VMEM((2, 2 * half), F32),
            pltpu.SemaphoreType.DMA((4,)),
        ],
        out_specs=[pl.BlockSpec(memory_space=pl.ANY)] * 3,
    )(got, slots, other, col, row, disp)
    return token_grads, param_grads, slot_output_grads


def solution(mesh):
    in_specs = (
        P(("group", "seq"), "exp"),
        P(("group", "seq"), "exp"),
        P(("group", "seq"), "exp"),
        P(("group", "seq", "exp"), None),
        P(("group", "seq", "exp"), None),
    )
    out_specs = (
        P(("group", "seq"), "exp"),
        P(("group", "seq"), "exp"),
        P(("group", "seq", "exp"), None),
    )
    return jax.shard_map(
        functools.partial(shards, mesh.shape["seq"]),
        mesh=mesh,
        in_specs=in_specs,
        out_specs=out_specs,
        check_vma=False,
    )
```

```python
import functools

import jax
import jax.numpy as jnp
from jax import lax
from jax.experimental import pallas as pl
from jax.experimental.pallas import tpu as pltpu
from jax.sharding import PartitionSpec as P

F32 = jnp.float32
BF16 = jnp.bfloat16
LONG = pl.CostEstimate(flops=10**10, bytes_accessed=10**7, transcendentals=0)


def dot(left, right):
    return jnp.dot(left, right, preferred_element_type=F32)


def dot_tn(left, right):
    return lax.dot_general(left, right, (((0,), (0,)), ((), ())), preferred_element_type=F32)


def call(kernel, outs, name, seq, scratch=(), **specs):
    return pl.pallas_call(
        kernel,
        out_shape=outs,
        scratch_shapes=list(scratch),
        compiler_params=pltpu.CompilerParams(vmem_limit_bytes=(16 if seq <= 16 else 48) << 20),
        name=name,
        **specs,
    )


def split16(value):
    high = value.astype(BF16).astype(F32)
    return high, (value - high).astype(BF16).astype(F32)


def seed_kernel(seed_ref):
    seed_ref[...] = jnp.zeros_like(seed_ref)


def pack_kernel(seed_ref, params_ref, outs_ref, grads_ref, chunks_ref):
    side = lax.axis_index("exp")
    half = params_ref.shape[1]
    quarter = half // 2

    def halves(ref):
        value = ref[...].astype(F32)
        first, second = value[:, :half], value[:, half:]
        return jnp.where(side == 0, first, second), jnp.where(side == 0, second, first)

    own, far = halves(outs_ref)
    pieces = (own[:, :quarter], own[:, quarter:], far[:, :quarter], far[:, quarter:])
    left = jnp.concatenate([params_ref[...].astype(F32), *halves(grads_ref)], axis=0).astype(BF16)
    right = jnp.concatenate(pieces, axis=0).astype(BF16)
    for dest in range(chunks_ref.shape[0]):
        chunks_ref[dest, :, :half] = left
        chunks_ref[dest, :, half:] = right


def products(slots_ref, tokens_ref, tokens_far_ref, upstream_ref, upstream_far_ref, side):
    seq, _, width = slots_ref.shape
    half = tokens_ref.shape[0]
    quarter = half // 2
    left = slots_ref[:, :, :half].reshape(8 * seq, half)
    right = slots_ref[:, :, half:].reshape(8 * seq, quarter)
    near, far = dot(left, tokens_ref[...]), dot(left, tokens_far_ref[...])
    by_quarter = [
        dot(right, ref[i * quarter : (i + 1) * quarter, :])
        for ref in (upstream_ref, upstream_far_ref)
        for i in range(2)
    ]
    row = lax.broadcasted_iota(jnp.int32, (8, near.shape[1]), 0)
    ours = row // 2 % 2 == side
    blocks = []
    for chip in range(0, seq, 2):
        parts = []
        for at in (8 * chip, 8 * chip + 8):
            one, two, three, four = (block[at : at + 8] for block in by_quarter)
            comb = jnp.where(row < 4, jnp.where(row < 2, one, two), jnp.where(row < 6, three, four))
            disp = jnp.where(row < 4, 0.0, jnp.where(row < 6, near[at : at + 8], far[at : at + 8]))
            comb, disp = comb + pltpu.roll(comb, 4, 0), disp + pltpu.roll(disp, 4, 0)
            comb, disp = comb + pltpu.roll(comb, 2, 0), disp + pltpu.roll(disp, 2, 0)
            parts.append((near[at : at + 8], comb, disp))
        (even, even_comb, even_disp), (odd, odd_comb, odd_disp) = parts
        logits = jnp.where(row < 4, even, pltpu.roll(odd, 4, 0))
        comb = jnp.where(ours, jnp.where(row < 4, even_comb, odd_comb), 0.0)
        disp = jnp.where(ours, jnp.where(row < 4, even_disp, odd_disp), 0.0)
        blocks.append((logits, comb, disp))
    return [jnp.concatenate(parts, axis=0) for parts in zip(*blocks)]


def near_kernel(slots_ref, *refs):
    side = lax.axis_index("exp")
    inputs, turned, part_refs = refs[:4], refs[4:8], refs[8:]
    for source, target in zip(inputs, turned):
        target[...] = source[...].T
    for ref, part in zip(part_refs, products(slots_ref, *turned, side)):
        ref[...] = part


def receiver(me, fours, step, four):
    return lax.bitwise_xor(me, step + 4 * four) if fours == 2 else 4 * four + lax.bitwise_xor(lax.rem(me, 4), step)


def crosses(fours, step, four):
    return (step > 0) != (fours == 2 and four > 0)


def local_kernel(
    slots_ref, tokens_ref, tokens_far_ref, upstream_ref, upstream_far_ref, *refs
):
    turned, (logit_ref, comb_ref, disp_ref), outs = refs[:4], refs[4:7], refs[7:]
    sends, (col_ref, row_ref, d_disp_ref) = outs[:4], outs[4:7]
    first_ref, second_ref, stats_ref, near_ref, far_ref = outs[7:]
    side, me = lax.axis_index("exp"), lax.axis_index("seq")
    n_slots, patches = col_ref.shape
    fours, _, width = sends[0].shape
    seq = 4 * fours
    half = tokens_ref.shape[1]
    extra = width - 2 * half
    groups = n_slots // 8 + 1
    parts = products(slots_ref, turned[1], turned[0], turned[3], turned[2], 1 - side)
    logits, d_comb, d_disp = (ref[...] + part for ref, part in zip((logit_ref, comb_ref, disp_ref), parts))
    row_exp = jnp.exp(logits - jnp.max(logits, axis=0, keepdims=True))
    combine = row_exp / jnp.sum(row_exp, axis=0, keepdims=True)
    row_part = combine * (d_comb - jnp.sum(combine * d_comb, axis=0, keepdims=True))
    top_high, top_low = split16(jnp.max(logits, axis=1, keepdims=True))
    col_exp = jnp.exp(logits - (top_high + top_low))
    sum_high, sum_low = split16(jnp.sum(col_exp, axis=1, keepdims=True))
    inner_high, inner_low = split16(jnp.sum(col_exp * d_disp, axis=1, keepdims=True))
    centre = (inner_high + inner_low) / (sum_high + sum_low)
    col_part = col_exp * (d_disp - centre)
    col_ref[...] = col_exp
    row_ref[...] = row_part
    d_disp_ref[...] = d_disp

    lane = lax.broadcasted_iota(jnp.int32, (n_slots, extra), 1)
    stats = jnp.zeros((n_slots, extra), F32)
    for j, stat in enumerate((top_high, top_low, sum_high, sum_low, inner_high, inner_low)):
        stats = jnp.where(lane == j * groups, stat, stats)
    every = jnp.zeros((8, extra), F32)
    for group in range(groups - 1):
        every = every + pltpu.roll(stats[8 * group : 8 * group + 8], group + 1, 1)

    row = lax.broadcasted_iota(jnp.int32, (8, patches), 0)
    for chip in range(0, seq, 2):
        span = slice(4 * chip, 4 * chip + 8)
        for ref, upper, lower in ((first_ref, combine, col_part), (second_ref, row_part, col_exp)):
            upper, lower = upper[span], lower[span]
            ref[chip] = jnp.where(row < 4, upper, pltpu.roll(lower, 4, 0))
            ref[chip + 1] = jnp.where(row < 4, pltpu.roll(upper, 4, 0), lower)
        own = stats[span]
        other = pltpu.roll(own, 4, 0)
        upper = lax.broadcasted_iota(jnp.int32, own.shape, 0) < 4
        stats_ref[chip] = every + jnp.where(upper, own, other)
        stats_ref[chip + 1] = every + jnp.where(upper, other, own)

    ours, theirs = (row // 2 == core for core in (side, 1 - side))
    for step in range(4):
        for four in range(fours):
            at = step * fours + four
            chip = receiver(me, fours, step, four)
            first, second = first_ref[chip], second_ref[chip]
            turned_first = jnp.where(row % 4 < 2, pltpu.roll(first, 6, 0), pltpu.roll(first, 2, 0))
            lower = jnp.where(row < 4, 0.0, first)
            here, there = (near_ref, far_ref) if not crosses(fours, step, four) else (far_ref, near_ref)
            direct, swapped = (first, turned_first) if not crosses(fours, step, four) else (turned_first, first)
            here[0, at], here[1, at] = lower, second
            there[0, at] = there[1, at] = jnp.zeros_like(lower)
            near_ref[2, at] = jnp.where(ours, direct, 0.0)
            far_ref[2, at] = jnp.where(theirs, swapped, 0.0)

    total = None
    for ref, token_half, upstream_half in ((near_ref, tokens_ref, upstream_ref), (far_ref, tokens_far_ref, upstream_far_ref)):
        rows = ref[...].reshape(3 * 8 * seq, patches).astype(BF16)
        by_tokens = dot(rows[: 16 * seq], token_half[...])
        left, right = by_tokens[: 8 * seq] + dot(rows[16 * seq :], upstream_half[...]), by_tokens[8 * seq :]
        total = (left, right) if total is None else (total[0] + left, total[1] + right)
    left, right = (value.reshape(4, fours, 8, half).astype(BF16) for value in total)
    for step, send_ref in enumerate(sends):
        send_ref[:, :, :half] = left[step]
        send_ref[:, :, half : 2 * half] = right[step]
        for four in range(fours):
            send_ref[four, :, 2 * half :] = stats_ref[receiver(me, fours, step, four)].astype(BF16)


def column_stats(stats, groups):
    extra = stats.shape[1]
    pair = stats + pltpu.roll(stats, extra - groups, 1)
    return pair, pltpu.roll(pair, extra - 2 * groups, 1), pltpu.roll(pair, extra - 4 * groups, 1)


def merge_stats(chunks, half, groups):
    blocks = [column_stats(chunk[:, 2 * half :].astype(F32), groups) for chunk in chunks]
    high = functools.reduce(jnp.maximum, [top for top, _, _ in blocks])
    scales = [jnp.exp(top - high) for top, _, _ in blocks]
    total = sum(scale * value for scale, (_, value, _) in zip(scales, blocks))
    inner = sum(scale * value for scale, (_, _, value) in zip(scales, blocks))
    return high, total, inner, scales, [inner / total for _, total, inner in blocks]


def merge_kernel(*refs, groups, half):
    chunk_refs, out_ref = refs[:4], refs[4]
    fours, _, width = chunk_refs[0].shape
    merged = out_ref.shape[0]
    lane = lax.broadcasted_iota(jnp.int32, (8, width - 2 * half), 1)
    upper = lax.broadcasted_iota(jnp.int32, lane.shape, 0) < 4
    for four in range(merged):
        chunks = [ref.at[four + fours - merged] for ref in chunk_refs]
        high, total, inner, scales, means = merge_stats(chunks, half, groups)
        stats = [part for stat in (high, total, inner) for part in split16(stat)]
        centre = (stats[4] + stats[5]) / (stats[2] + stats[3])
        left = right = jnp.zeros((8, half), F32)
        for chunk, scale, mean in zip(chunks, scales, means):
            weight = jnp.where(upper, 1.0, scale)[:, 0:1]
            moved = jnp.where(upper, 0.0, scale * (mean - centre))[:, 0:1]
            by_right = chunk[:, half : 2 * half].astype(F32)
            left = left + weight * chunk[:, :half].astype(F32) + moved * by_right
            right = right + weight * by_right
        out_ref[four, :, :half] = left.astype(BF16)
        out_ref[four, :, half : 2 * half] = right.astype(BF16)
        block = sum(pltpu.roll(jnp.where(lane < groups, stat, 0.0), j * groups, 1) for j, stat in enumerate(stats))
        out_ref[four, :, 2 * half :] = block.astype(BF16)


def finish_kernel(*refs):
    inputs, outs_and_scratch = refs[:-8], refs[-8:]
    slots_ref, other_ref, col_ref, row_ref, disp_ref, mine_ref, *rest = inputs
    params_out, tokens_out, sums_out, rows_ref, params_ref, tokens_ref, sums_ref, sems = outs_and_scratch
    side = lax.axis_index("exp")
    half = params_ref.shape[1]
    seq = slots_ref.shape[0]
    n_slots = col_ref.shape[0]
    groups = n_slots // 8 + 1
    if seq == 8:
        chunks = [ref.at[0] for ref in (mine_ref, *rest)]
    else:
        chunks = [rest[0].at[four] for four in range(rest[0].shape[0])]
    high, total, inner, scales, means = merge_stats(chunks, half, groups)
    centre = inner / total

    top, _, _ = column_stats(mine_ref[0, :, 2 * half :].astype(F32), groups)
    weight = jnp.exp(top - high) / total
    zero = jnp.zeros((6, col_ref.shape[1]), F32)
    for group in range(groups - 1):
        span = slice(8 * group, 8 * group + 8)
        dispatch = col_ref[span] * weight[:, group + 1 : group + 2]
        d_logit = row_ref[span] + dispatch * (disp_ref[span] - centre[:, group + 1 : group + 2])
        first = jnp.where(side == 0, dispatch, pltpu.roll(dispatch, 6, 0))
        second = jnp.where(side == 0, pltpu.roll(dispatch, 6, 0), dispatch)
        for j in range(2):
            span = slice(16 * group + 8 * j, 16 * group + 8 * j + 8)
            ours, theirs = first[4 * j : 4 * j + 2], second[4 * j : 4 * j + 2]
            rows_ref[0, span, :] = jnp.concatenate([d_logit[4 * j : 4 * j + 4], ours, zero[0:2]], axis=0)
            rows_ref[1, span, :] = jnp.concatenate([zero, theirs], axis=0)
    left = rows_ref[...].reshape(16 * seq, -1).astype(BF16)
    right = jnp.concatenate([ref[:, :, :half].reshape(8 * seq, half) for ref in (slots_ref, other_ref)], axis=0)
    patches = tokens_ref.shape[0] // 2
    copies = []
    for part in range(2):
        span = slice(part * patches, (part + 1) * patches)
        tokens_ref[span, :] = dot_tn(left[:, span], right).astype(BF16)
        copies.append(pltpu.make_async_copy(tokens_ref.at[span], tokens_out.at[span], sems.at[part]))
        copies[-1].start()

    upper = lax.broadcasted_iota(jnp.int32, centre.shape, 0) < 4
    left = right = jnp.zeros((8, half), F32)
    for chunk, scale, mean in zip(chunks, scales, means):
        weight = scale / total
        by_left = jnp.where(upper, 1.0, weight)
        by_right = jnp.where(upper, 1.0, weight * (mean - centre))
        left = left + by_left[:, 0:1] * chunk[:, :half].astype(F32)
        right = right + by_right[:, 0:1] * chunk[:, half : 2 * half].astype(F32)
    sums_ref[:, :half] = left[0:2]
    sums_ref[:, half:] = left[2:4]
    params_ref[...] = left[4:8] + right[0:4] + right[4:8]
    for i, (source, target) in enumerate(((params_ref, params_out), (sums_ref, sums_out))):
        copies.append(pltpu.make_async_copy(source, target, sems.at[2 + i]))
        copies[-1].start()
    for copy in copies:
        copy.wait()


def to_other_core(value, seq, step):
    pairs = [(2 * chip + core, 2 * (chip ^ step) + 1 - core) for chip in range(seq) for core in range(2)]
    return lax.ppermute(value, ("seq", "exp"), pairs)


def shards(seq, tokens, upstream, slot_params, slot_outputs, slot_input_grads):
    patches, half = tokens.shape
    n_slots = slot_params.shape[0] * seq
    extra = -(-6 * (n_slots // 8 + 1) // 128) * 128
    sds = jax.ShapeDtypeStruct
    cores = [(0, 1), (1, 0)]

    tokens_far, far = (lax.ppermute(x, "exp", cores) for x in (tokens, upstream))
    seed = call(seed_kernel, sds((8, 128), F32), "seed", seq, cost_estimate=LONG)()
    chunks = call(pack_kernel, sds((seq, 8, half + half // 2), BF16), "pack", seq)(
        seed, slot_params, slot_outputs, slot_input_grads
    )
    slots = lax.all_to_all(chunks, "seq", split_axis=0, concat_axis=0, tiled=True)
    other = lax.ppermute(slots, "exp", cores)
    by_slot = sds((n_slots, patches), F32)
    turned = sds((half, patches), BF16)
    near = call(near_kernel, (turned,) * 4 + (by_slot,) * 3, "near", seq, cost_estimate=LONG)(
        slots, tokens, tokens_far, upstream, far
    )
    fours = seq // 4
    chunk = (8, 2 * half + extra)
    *sends, col, row, disp = call(
        local_kernel,
        (sds((fours, *chunk), BF16),) * 4 + (by_slot,) * 3,
        "local",
        seq,
        [pltpu.VMEM((seq, 8, patches), F32)] * 2
        + [pltpu.VMEM((seq, 8, extra), F32)]
        + [pltpu.VMEM((3, seq, 8, patches), F32)] * 2,
    )(other, tokens, tokens_far, upstream, far, *near)
    got = [sends[0]] + [to_other_core(sends[step], seq, step) for step in range(1, 4)]
    merged = call(
        functools.partial(merge_kernel, groups=n_slots // 8 + 1, half=half),
        sds((1 if fours == 2 else fours, *chunk), BF16),
        "merge",
        seq,
    )(*got)
    if fours == 2:
        got.append(to_other_core(merged, seq, 4))
    else:
        same = [[4 * four + step for four in range(fours)] for step in range(4)]
        got[1:] = [lax.all_to_all(merged, "seq", split_axis=0, concat_axis=0, tiled=True, axis_index_groups=same)]
    param_grads, token_grads, slot_output_grads = call(
        finish_kernel,
        (sds((4, half), F32), sds((patches, half), BF16), sds((2, 2 * half), F32)),
        "finish",
        seq,
        [
            pltpu.VMEM((2, 8 * seq, patches), F32),
            pltpu.VMEM((4, half), F32),
            pltpu.VMEM((patches, half), BF16),
            pltpu.VMEM((2, 2 * half), F32),
            pltpu.SemaphoreType.DMA((4,)),
        ],
        out_specs=[pl.BlockSpec(memory_space=pl.ANY)] * 3,
    )(slots, other, col, row, disp, *got)
    return token_grads, param_grads, slot_output_grads


def solution(mesh):
    in_specs = (
        P(("group", "seq"), "exp"),
        P(("group", "seq"), "exp"),
        P(("group", "seq"), "exp"),
        P(("group", "seq", "exp"), None),
        P(("group", "seq", "exp"), None),
    )
    out_specs = (
        P(("group", "seq"), "exp"),
        P(("group", "seq"), "exp"),
        P(("group", "seq", "exp"), None),
    )
    return jax.shard_map(
        functools.partial(shards, mesh.shape["seq"]),
        mesh=mesh,
        in_specs=in_specs,
        out_specs=out_specs,
        check_vma=False,
    )
```

```python
import functools

import jax
import jax.numpy as jnp
from jax import lax
from jax.experimental import pallas as pl
from jax.experimental.pallas import tpu as pltpu
from jax.sharding import PartitionSpec as P

F32 = jnp.float32
BF16 = jnp.bfloat16
LONG = pl.CostEstimate(flops=10**10, bytes_accessed=10**7, transcendentals=0)


def dot(left, right):
    return jnp.dot(left, right, preferred_element_type=F32)


def dot_tn(left, right):
    return lax.dot_general(left, right, (((0,), (0,)), ((), ())), preferred_element_type=F32)


def call(kernel, outs, name, seq, scratch=(), **specs):
    return pl.pallas_call(
        kernel,
        out_shape=outs,
        scratch_shapes=list(scratch),
        compiler_params=pltpu.CompilerParams(vmem_limit_bytes=(16 if seq <= 16 else 48) << 20),
        name=name,
        **specs,
    )


def split16(value):
    high = value.astype(BF16).astype(F32)
    return high, (value - high).astype(BF16).astype(F32)


def receiver(me, fours, step, four):
    return lax.bitwise_xor(me, step + 4 * four) if fours == 2 else 4 * four + lax.bitwise_xor(lax.rem(me, 4), step)


def crosses(fours, step, four):
    return (step > 0) != (fours == 2 and four > 0)


def seed_kernel(seed_ref):
    seed_ref[...] = jnp.zeros_like(seed_ref)


def pack_kernel(seed_ref, params_ref, outs_ref, grads_ref, chunks_ref):
    side = lax.axis_index("exp")
    half = params_ref.shape[1]
    quarter = half // 2

    def halves(ref):
        value = ref[...].astype(F32)
        first, second = value[:, :half], value[:, half:]
        return jnp.where(side == 0, first, second), jnp.where(side == 0, second, first)

    own, far = halves(outs_ref)
    pieces = (own[:, :quarter], own[:, quarter:], far[:, :quarter], far[:, quarter:])
    left = jnp.concatenate([params_ref[...].astype(F32), *halves(grads_ref)], axis=0).astype(BF16)
    right = jnp.concatenate(pieces, axis=0).astype(BF16)
    for dest in range(chunks_ref.shape[0]):
        chunks_ref[dest, :, :half] = left
        chunks_ref[dest, :, half:] = right


def pair_kernel(mine_ref, taken_ref, pair_ref):
    pair_ref[0:1] = mine_ref[...]
    pair_ref[1:2] = taken_ref[...]


def order_kernel(*refs):
    me = lax.axis_index("seq")
    *piece_refs, slots_ref = refs
    for step, piece_ref in enumerate(piece_refs):
        for four in range(2):
            slots_ref[receiver(me, 2, step, four)] = piece_ref[four]


def owner(chip, seq):
    side = lax.axis_index("exp")
    if seq != 8:
        return side
    path = lax.bitwise_xor(chip, lax.axis_index("seq"))
    return lax.rem(side + (lax.rem(path, 4) > 0).astype(jnp.int32) + path // 4, 2)


def products(slots_ref, tokens_ref, tokens_far_ref, upstream_ref, upstream_far_ref, cores):
    side = lax.axis_index("exp")
    seq, _, width = slots_ref.shape
    half = tokens_ref.shape[0]
    quarter = half // 2
    left = slots_ref[:, :, :half].reshape(8 * seq, half)
    right = slots_ref[:, :, half:].reshape(8 * seq, quarter)
    near, far = dot(left, tokens_ref[...]), dot(left, tokens_far_ref[...])
    by_quarter = [
        dot(right, ref[i * quarter : (i + 1) * quarter, :])
        for ref in (upstream_ref, upstream_far_ref)
        for i in range(2)
    ]
    row = lax.broadcasted_iota(jnp.int32, (8, near.shape[1]), 0)
    blocks = []
    for chip in range(0, seq, 2):
        parts = []
        for core, at in ((cores[chip], 8 * chip), (cores[chip + 1], 8 * chip + 8)):
            direct = core == side
            one, two, three, four, same, cross = (block[at : at + 8] for block in (*by_quarter, near, far))
            one, three = jnp.where(direct, one, three), jnp.where(direct, three, one)
            two, four = jnp.where(direct, two, four), jnp.where(direct, four, two)
            same, cross = jnp.where(direct, same, cross), jnp.where(direct, cross, same)
            comb = jnp.where(row < 4, jnp.where(row < 2, one, two), jnp.where(row < 6, three, four))
            disp = jnp.where(row < 4, 0.0, jnp.where(row < 6, same, cross))
            comb, disp = comb + pltpu.roll(comb, 4, 0), disp + pltpu.roll(disp, 4, 0)
            comb, disp = comb + pltpu.roll(comb, 2, 0), disp + pltpu.roll(disp, 2, 0)
            ours = row // 2 % 2 == core
            parts.append((same, jnp.where(ours, comb, 0.0), jnp.where(ours, disp, 0.0)))
        (even, even_comb, even_disp), (odd, odd_comb, odd_disp) = parts
        logits = jnp.where(row < 4, even, pltpu.roll(odd, 4, 0))
        blocks.append((logits, jnp.where(row < 4, even_comb, odd_comb), jnp.where(row < 4, even_disp, odd_disp)))
    return [jnp.concatenate(parts, axis=0) for parts in zip(*blocks)]


def near_kernel(slots_ref, *refs):
    inputs, turned, part_refs = refs[:4], refs[4:8], refs[8:]
    seq = slots_ref.shape[0]
    for source, target in zip(inputs, turned):
        target[...] = source[...].T
    cores = [owner(chip, seq) for chip in range(seq)]
    for ref, part in zip(part_refs, products(slots_ref, *turned, cores)):
        ref[...] = part


def local_kernel(
    slots_ref, tokens_ref, tokens_far_ref, upstream_ref, upstream_far_ref, *refs
):
    turned, (logit_ref, comb_ref, disp_ref), outs = refs[:4], refs[4:7], refs[7:]
    sends, (col_ref, row_ref, d_disp_ref) = outs[:4], outs[4:7]
    first_ref, second_ref, stats_ref, near_ref, far_ref = outs[7:]
    side, me = lax.axis_index("exp"), lax.axis_index("seq")
    n_slots, patches = col_ref.shape
    fours, _, width = sends[0].shape
    seq = 4 * fours
    half = tokens_ref.shape[1]
    extra = width - 2 * half
    groups = n_slots // 8 + 1
    parts = products(slots_ref, *turned, [1 - owner(chip, seq) for chip in range(seq)])
    logits, d_comb, d_disp = (ref[...] + part for ref, part in zip((logit_ref, comb_ref, disp_ref), parts))
    row_exp = jnp.exp(logits - jnp.max(logits, axis=0, keepdims=True))
    combine = row_exp / jnp.sum(row_exp, axis=0, keepdims=True)
    row_part = combine * (d_comb - jnp.sum(combine * d_comb, axis=0, keepdims=True))
    top_high, top_low = split16(jnp.max(logits, axis=1, keepdims=True))
    col_exp = jnp.exp(logits - (top_high + top_low))
    sum_high, sum_low = split16(jnp.sum(col_exp, axis=1, keepdims=True))
    inner_high, inner_low = split16(jnp.sum(col_exp * d_disp, axis=1, keepdims=True))
    centre = (inner_high + inner_low) / (sum_high + sum_low)
    col_part = col_exp * (d_disp - centre)
    col_ref[...] = col_exp
    row_ref[...] = row_part
    d_disp_ref[...] = d_disp

    lane = lax.broadcasted_iota(jnp.int32, (n_slots, extra), 1)
    stats = jnp.zeros((n_slots, extra), F32)
    for j, stat in enumerate((top_high, top_low, sum_high, sum_low, inner_high, inner_low)):
        stats = jnp.where(lane == j * groups, stat, stats)
    every = jnp.zeros((8, extra), F32)
    for group in range(groups - 1):
        every = every + pltpu.roll(stats[8 * group : 8 * group + 8], group + 1, 1)

    row = lax.broadcasted_iota(jnp.int32, (8, patches), 0)
    for chip in range(0, seq, 2):
        span = slice(4 * chip, 4 * chip + 8)
        for ref, upper, lower in ((first_ref, combine, col_part), (second_ref, row_part, col_exp)):
            upper, lower = upper[span], lower[span]
            ref[chip] = jnp.where(row < 4, upper, pltpu.roll(lower, 4, 0))
            ref[chip + 1] = jnp.where(row < 4, pltpu.roll(upper, 4, 0), lower)
        own = stats[span]
        other = pltpu.roll(own, 4, 0)
        upper = lax.broadcasted_iota(jnp.int32, own.shape, 0) < 4
        stats_ref[chip] = every + jnp.where(upper, own, other)
        stats_ref[chip + 1] = every + jnp.where(upper, other, own)

    ours, theirs = (row // 2 == core for core in (side, 1 - side))
    for step in range(4):
        for four in range(fours):
            at = step * fours + four
            chip = receiver(me, fours, step, four)
            first, second = first_ref[chip], second_ref[chip]
            turned_first = jnp.where(row % 4 < 2, pltpu.roll(first, 6, 0), pltpu.roll(first, 2, 0))
            lower = jnp.where(row < 4, 0.0, first)
            here, there = (near_ref, far_ref) if not crosses(fours, step, four) else (far_ref, near_ref)
            direct, swapped = (first, turned_first) if not crosses(fours, step, four) else (turned_first, first)
            here[0, at], here[1, at] = lower, second
            there[0, at] = there[1, at] = jnp.zeros_like(lower)
            near_ref[2, at] = jnp.where(ours, direct, 0.0)
            far_ref[2, at] = jnp.where(theirs, swapped, 0.0)

    total = None
    for ref, token_half, upstream_half in ((near_ref, tokens_ref, upstream_ref), (far_ref, tokens_far_ref, upstream_far_ref)):
        rows = ref[...].reshape(3 * 8 * seq, patches).astype(BF16)
        by_tokens = dot(rows[: 16 * seq], token_half[...])
        left, right = by_tokens[: 8 * seq] + dot(rows[16 * seq :], upstream_half[...]), by_tokens[8 * seq :]
        total = (left, right) if total is None else (total[0] + left, total[1] + right)
    left, right = (value.reshape(4, fours, 8, half).astype(BF16) for value in total)
    for step, send_ref in enumerate(sends):
        send_ref[:, :, :half] = left[step]
        send_ref[:, :, half : 2 * half] = right[step]
        for four in range(fours):
            send_ref[four, :, 2 * half :] = stats_ref[receiver(me, fours, step, four)].astype(BF16)


def column_stats(stats, groups):
    extra = stats.shape[1]
    pair = stats + pltpu.roll(stats, extra - groups, 1)
    return pair, pltpu.roll(pair, extra - 2 * groups, 1), pltpu.roll(pair, extra - 4 * groups, 1)


def merge_stats(chunks, half, groups):
    blocks = [column_stats(chunk[:, 2 * half :].astype(F32), groups) for chunk in chunks]
    high = functools.reduce(jnp.maximum, [top for top, _, _ in blocks])
    scales = [jnp.exp(top - high) for top, _, _ in blocks]
    total = sum(scale * value for scale, (_, value, _) in zip(scales, blocks))
    inner = sum(scale * value for scale, (_, _, value) in zip(scales, blocks))
    return high, total, inner, scales, [inner / total for _, total, inner in blocks]


def merge_kernel(*refs, groups, half):
    chunk_refs, out_ref = refs[:4], refs[4]
    fours, _, width = chunk_refs[0].shape
    merged = out_ref.shape[0]
    lane = lax.broadcasted_iota(jnp.int32, (8, width - 2 * half), 1)
    upper = lax.broadcasted_iota(jnp.int32, lane.shape, 0) < 4
    for four in range(merged):
        chunks = [ref.at[four + fours - merged] for ref in chunk_refs]
        high, total, inner, scales, means = merge_stats(chunks, half, groups)
        stats = [part for stat in (high, total, inner) for part in split16(stat)]
        centre = (stats[4] + stats[5]) / (stats[2] + stats[3])
        left = right = jnp.zeros((8, half), F32)
        for chunk, scale, mean in zip(chunks, scales, means):
            weight = jnp.where(upper, 1.0, scale)[:, 0:1]
            moved = jnp.where(upper, 0.0, scale * (mean - centre))[:, 0:1]
            by_right = chunk[:, half : 2 * half].astype(F32)
            left = left + weight * chunk[:, :half].astype(F32) + moved * by_right
            right = right + weight * by_right
        out_ref[four, :, :half] = left.astype(BF16)
        out_ref[four, :, half : 2 * half] = right.astype(BF16)
        block = sum(pltpu.roll(jnp.where(lane < groups, stat, 0.0), j * groups, 1) for j, stat in enumerate(stats))
        out_ref[four, :, 2 * half :] = block.astype(BF16)


def finish_kernel(*refs):
    inputs, outs_and_scratch = refs[:-8], refs[-8:]
    slots_ref, other_ref, col_ref, row_ref, disp_ref, mine_ref, *rest = inputs
    params_out, tokens_out, sums_out, rows_ref, params_ref, tokens_ref, sums_ref, sems = outs_and_scratch
    side = lax.axis_index("exp")
    half = params_ref.shape[1]
    seq = slots_ref.shape[0]
    n_slots = col_ref.shape[0]
    groups = n_slots // 8 + 1
    if seq == 8:
        chunks = [ref.at[0] for ref in (mine_ref, *rest)]
    else:
        chunks = [rest[0].at[four] for four in range(rest[0].shape[0])]
    high, total, inner, scales, means = merge_stats(chunks, half, groups)
    centre = inner / total

    top, _, _ = column_stats(mine_ref[0, :, 2 * half :].astype(F32), groups)
    weight = jnp.exp(top - high) / total
    zero = jnp.zeros((6, col_ref.shape[1]), F32)
    for group in range(groups - 1):
        span = slice(8 * group, 8 * group + 8)
        dispatch = col_ref[span] * weight[:, group + 1 : group + 2]
        d_logit = row_ref[span] + dispatch * (disp_ref[span] - centre[:, group + 1 : group + 2])
        first = jnp.where(side == 0, dispatch, pltpu.roll(dispatch, 6, 0))
        second = jnp.where(side == 0, pltpu.roll(dispatch, 6, 0), dispatch)
        for j in range(2):
            span = slice(16 * group + 8 * j, 16 * group + 8 * j + 8)
            ahead = lax.rem(owner(2 * group + j, seq) + side, 2)
            ours, theirs = first[4 * j : 4 * j + 2], second[4 * j : 4 * j + 2]
            rows_ref[ahead, span, :] = jnp.concatenate([d_logit[4 * j : 4 * j + 4], ours, zero[0:2]], axis=0)
            rows_ref[1 - ahead, span, :] = jnp.concatenate([zero, theirs], axis=0)
    left = rows_ref[...].reshape(16 * seq, -1).astype(BF16)
    right = jnp.concatenate([ref[:, :, :half].reshape(8 * seq, half) for ref in (slots_ref, other_ref)], axis=0)
    patches = tokens_ref.shape[0] // 2
    copies = []
    for part in range(2):
        span = slice(part * patches, (part + 1) * patches)
        tokens_ref[span, :] = dot_tn(left[:, span], right).astype(BF16)
        copies.append(pltpu.make_async_copy(tokens_ref.at[span], tokens_out.at[span], sems.at[part]))
        copies[-1].start()

    upper = lax.broadcasted_iota(jnp.int32, centre.shape, 0) < 4
    left = right = jnp.zeros((8, half), F32)
    for chunk, scale, mean in zip(chunks, scales, means):
        weight = scale / total
        by_left = jnp.where(upper, 1.0, weight)
        by_right = jnp.where(upper, 1.0, weight * (mean - centre))
        left = left + by_left[:, 0:1] * chunk[:, :half].astype(F32)
        right = right + by_right[:, 0:1] * chunk[:, half : 2 * half].astype(F32)
    sums_ref[:, :half] = left[0:2]
    sums_ref[:, half:] = left[2:4]
    params_ref[...] = left[4:8] + right[0:4] + right[4:8]
    for i, (source, target) in enumerate(((params_ref, params_out), (sums_ref, sums_out))):
        copies.append(pltpu.make_async_copy(source, target, sems.at[2 + i]))
        copies[-1].start()
    for copy in copies:
        copy.wait()


def to_other_core(value, seq, step):
    pairs = [(2 * chip + core, 2 * (chip ^ step) + 1 - core) for chip in range(seq) for core in range(2)]
    return lax.ppermute(value, ("seq", "exp"), pairs)


def shards(seq, tokens, upstream, slot_params, slot_outputs, slot_input_grads):
    patches, half = tokens.shape
    n_slots = slot_params.shape[0] * seq
    extra = -(-6 * (n_slots // 8 + 1) // 128) * 128
    sds = jax.ShapeDtypeStruct
    cores = [(0, 1), (1, 0)]

    tokens_far, far = (lax.ppermute(x, "exp", cores) for x in (tokens, upstream))
    seed = call(seed_kernel, sds((8, 128), F32), "seed", seq, cost_estimate=LONG)()
    fours = seq // 4
    rows = (8, half + half // 2)
    chunks = call(pack_kernel, sds((1 if fours == 2 else seq, *rows), BF16), "pack", seq)(
        seed, slot_params, slot_outputs, slot_input_grads
    )
    if fours == 2:
        taken = to_other_core(chunks, seq, 4)
        pieces = [call(pair_kernel, sds((2, *rows), BF16), "pair", seq)(chunks, taken)]
        pieces += [to_other_core(pieces[0], seq, step) for step in range(1, 4)]
        slots = call(order_kernel, sds((seq, *rows), BF16), "order", seq)(*pieces)
    else:
        slots = lax.all_to_all(chunks, "seq", split_axis=0, concat_axis=0, tiled=True)
    other = lax.ppermute(slots, "exp", cores)
    by_slot = sds((n_slots, patches), F32)
    turned = sds((half, patches), BF16)
    near = call(near_kernel, (turned,) * 4 + (by_slot,) * 3, "near", seq, cost_estimate=LONG)(
        slots, tokens, tokens_far, upstream, far
    )
    chunk = (8, 2 * half + extra)
    *sends, col, row, disp = call(
        local_kernel,
        (sds((fours, *chunk), BF16),) * 4 + (by_slot,) * 3,
        "local",
        seq,
        [pltpu.VMEM((seq, 8, patches), F32)] * 2
        + [pltpu.VMEM((seq, 8, extra), F32)]
        + [pltpu.VMEM((3, seq, 8, patches), F32)] * 2,
    )(other, tokens, tokens_far, upstream, far, *near)
    got = [sends[0]] + [to_other_core(sends[step], seq, step) for step in range(1, 4)]
    merged = call(
        functools.partial(merge_kernel, groups=n_slots // 8 + 1, half=half),
        sds((1 if fours == 2 else fours, *chunk), BF16),
        "merge",
        seq,
    )(*got)
    if fours == 2:
        got.append(to_other_core(merged, seq, 4))
    else:
        same = [[4 * four + step for four in range(fours)] for step in range(4)]
        got[1:] = [lax.all_to_all(merged, "seq", split_axis=0, concat_axis=0, tiled=True, axis_index_groups=same)]
    param_grads, token_grads, slot_output_grads = call(
        finish_kernel,
        (sds((4, half), F32), sds((patches, half), BF16), sds((2, 2 * half), F32)),
        "finish",
        seq,
        [
            pltpu.VMEM((2, 8 * seq, patches), F32),
            pltpu.VMEM((4, half), F32),
            pltpu.VMEM((patches, half), BF16),
            pltpu.VMEM((2, 2 * half), F32),
            pltpu.SemaphoreType.DMA((4,)),
        ],
        out_specs=[pl.BlockSpec(memory_space=pl.ANY)] * 3,
    )(slots, other, col, row, disp, *got)
    return token_grads, param_grads, slot_output_grads


def solution(mesh):
    in_specs = (
        P(("group", "seq"), "exp"),
        P(("group", "seq"), "exp"),
        P(("group", "seq"), "exp"),
        P(("group", "seq", "exp"), None),
        P(("group", "seq", "exp"), None),
    )
    out_specs = (
        P(("group", "seq"), "exp"),
        P(("group", "seq"), "exp"),
        P(("group", "seq", "exp"), None),
    )
    return jax.shard_map(
        functools.partial(shards, mesh.shape["seq"]),
        mesh=mesh,
        in_specs=in_specs,
        out_specs=out_specs,
        check_vma=False,
    )
```

```python
import functools

import jax
import jax.numpy as jnp
from jax import lax
from jax.experimental import pallas as pl
from jax.experimental.pallas import tpu as pltpu
from jax.sharding import PartitionSpec as P

F32 = jnp.float32
BF16 = jnp.bfloat16
LONG = pl.CostEstimate(flops=10**10, bytes_accessed=10**7, transcendentals=0)


def dot(left, right):
    return jnp.dot(left, right, preferred_element_type=F32)


def dot_tn(left, right):
    return lax.dot_general(left, right, (((0,), (0,)), ((), ())), preferred_element_type=F32)


def call(kernel, outs, name, seq, scratch=(), **specs):
    return pl.pallas_call(
        kernel,
        out_shape=outs,
        scratch_shapes=list(scratch),
        compiler_params=pltpu.CompilerParams(vmem_limit_bytes=(16 if seq <= 16 else 48) << 20),
        name=name,
        **specs,
    )


def split16(value):
    high = value.astype(BF16).astype(F32)
    return high, (value - high).astype(BF16).astype(F32)


def receiver(me, fours, step, four):
    return lax.bitwise_xor(me, step + 4 * four) if fours == 2 else 4 * four + lax.bitwise_xor(lax.rem(me, 4), step)


def crosses(fours, step, four):
    return (step > 0) != (fours == 2 and four > 0)


def seed_kernel(seed_ref):
    seed_ref[...] = jnp.zeros_like(seed_ref)


def pack_kernel(seed_ref, params_ref, outs_ref, grads_ref, chunks_ref):
    side = lax.axis_index("exp")
    half = params_ref.shape[1]
    quarter = half // 2

    def halves(ref):
        value = ref[...].astype(F32)
        first, second = value[:, :half], value[:, half:]
        return jnp.where(side == 0, first, second), jnp.where(side == 0, second, first)

    own, far = halves(outs_ref)
    pieces = (own[:, :quarter], own[:, quarter:], far[:, :quarter], far[:, quarter:])
    left = jnp.concatenate([params_ref[...].astype(F32), *halves(grads_ref)], axis=0).astype(BF16)
    right = jnp.concatenate(pieces, axis=0).astype(BF16)
    for dest in range(chunks_ref.shape[0]):
        chunks_ref[dest, :, :half] = left
        chunks_ref[dest, :, half:] = right


def pair_kernel(mine_ref, taken_ref, pair_ref):
    pair_ref[0:1] = mine_ref[...]
    pair_ref[1:2] = taken_ref[...]


def order_kernel(*refs):
    me = lax.axis_index("seq")
    *piece_refs, slots_ref = refs
    for step, piece_ref in enumerate(piece_refs):
        for four in range(2):
            slots_ref[receiver(me, 2, step, four)] = piece_ref[four]


def owner(chip, seq):
    side = lax.axis_index("exp")
    if seq != 8:
        return side
    path = lax.bitwise_xor(chip, lax.axis_index("seq"))
    return lax.rem(side + (lax.rem(path, 4) > 0).astype(jnp.int32) + path // 4, 2)


def products(slots_ref, tokens_ref, tokens_far_ref, upstream_ref, upstream_far_ref, cores):
    side = lax.axis_index("exp")
    seq, _, width = slots_ref.shape
    half = tokens_ref.shape[0]
    quarter = half // 2
    left = slots_ref[:, :, :half].reshape(8 * seq, half)
    right = slots_ref[:, :, half:].reshape(8 * seq, quarter)
    near, far = dot(left, tokens_ref[...]), dot(left, tokens_far_ref[...])
    by_quarter = [
        dot(right, ref[i * quarter : (i + 1) * quarter, :])
        for ref in (upstream_ref, upstream_far_ref)
        for i in range(2)
    ]
    row = lax.broadcasted_iota(jnp.int32, (8, near.shape[1]), 0)
    blocks = []
    for chip in range(0, seq, 2):
        parts = []
        for core, at in ((cores[chip], 8 * chip), (cores[chip + 1], 8 * chip + 8)):
            direct = core == side
            one, two, three, four, same, cross = (block[at : at + 8] for block in (*by_quarter, near, far))
            one, three = jnp.where(direct, one, three), jnp.where(direct, three, one)
            two, four = jnp.where(direct, two, four), jnp.where(direct, four, two)
            same, cross = jnp.where(direct, same, cross), jnp.where(direct, cross, same)
            comb = jnp.where(row < 4, jnp.where(row < 2, one, two), jnp.where(row < 6, three, four))
            disp = jnp.where(row < 4, 0.0, jnp.where(row < 6, same, cross))
            comb, disp = comb + pltpu.roll(comb, 4, 0), disp + pltpu.roll(disp, 4, 0)
            comb, disp = comb + pltpu.roll(comb, 2, 0), disp + pltpu.roll(disp, 2, 0)
            ours = row // 2 % 2 == core
            parts.append((same, jnp.where(ours, comb, 0.0), jnp.where(ours, disp, 0.0)))
        (even, even_comb, even_disp), (odd, odd_comb, odd_disp) = parts
        logits = jnp.where(row < 4, even, pltpu.roll(odd, 4, 0))
        blocks.append((logits, jnp.where(row < 4, even_comb, odd_comb), jnp.where(row < 4, even_disp, odd_disp)))
    return [jnp.concatenate(parts, axis=0) for parts in zip(*blocks)]


def near_kernel(slots_ref, *refs):
    inputs, turned, part_refs = refs[:4], refs[4:8], refs[8:]
    seq = slots_ref.shape[0]
    for source, target in zip(inputs, turned):
        target[...] = source[...].T
    cores = [owner(chip, seq) for chip in range(seq)]
    for ref, part in zip(part_refs, products(slots_ref, *turned, cores)):
        ref[...] = part


def local_kernel(
    slots_ref, tokens_ref, tokens_far_ref, upstream_ref, upstream_far_ref, *refs
):
    turned, (logit_ref, comb_ref, disp_ref), outs = refs[:4], refs[4:7], refs[7:]
    sends, (col_ref, row_ref, d_disp_ref) = outs[:4], outs[4:7]
    first_ref, second_ref, stats_ref, near_ref, far_ref = outs[7:]
    side, me = lax.axis_index("exp"), lax.axis_index("seq")
    n_slots, patches = col_ref.shape
    fours, _, width = sends[0].shape
    seq = 4 * fours
    half = tokens_ref.shape[1]
    extra = width - 2 * half
    groups = n_slots // 8 + 1
    parts = products(slots_ref, *turned, [1 - owner(chip, seq) for chip in range(seq)])
    logits, d_comb, d_disp = (ref[...] + part for ref, part in zip((logit_ref, comb_ref, disp_ref), parts))
    row_exp = jnp.exp(logits - jnp.max(logits, axis=0, keepdims=True))
    combine = row_exp / jnp.sum(row_exp, axis=0, keepdims=True)
    row_part = combine * (d_comb - jnp.sum(combine * d_comb, axis=0, keepdims=True))
    top_high, top_low = split16(jnp.max(logits, axis=1, keepdims=True))
    col_exp = jnp.exp(logits - (top_high + top_low))
    sum_high, sum_low = split16(jnp.sum(col_exp, axis=1, keepdims=True))
    inner_high, inner_low = split16(jnp.sum(col_exp * d_disp, axis=1, keepdims=True))
    centre = (inner_high + inner_low) / (sum_high + sum_low)
    col_part = col_exp * (d_disp - centre)
    col_ref[...] = col_exp
    row_ref[...] = row_part
    d_disp_ref[...] = d_disp

    lane = lax.broadcasted_iota(jnp.int32, (n_slots, extra), 1)
    stats = jnp.zeros((n_slots, extra), F32)
    for j, stat in enumerate((top_high, top_low, sum_high, sum_low, inner_high, inner_low)):
        stats = jnp.where(lane == j * groups, stat, stats)
    every = jnp.zeros((8, extra), F32)
    for group in range(groups - 1):
        every = every + pltpu.roll(stats[8 * group : 8 * group + 8], group + 1, 1)

    row = lax.broadcasted_iota(jnp.int32, (8, patches), 0)
    for chip in range(0, seq, 2):
        span = slice(4 * chip, 4 * chip + 8)
        for ref, upper, lower in ((first_ref, combine, col_part), (second_ref, row_part, col_exp)):
            upper, lower = upper[span], lower[span]
            ref[chip] = jnp.where(row < 4, upper, pltpu.roll(lower, 4, 0))
            ref[chip + 1] = jnp.where(row < 4, pltpu.roll(upper, 4, 0), lower)
        own = stats[span]
        other = pltpu.roll(own, 4, 0)
        upper = lax.broadcasted_iota(jnp.int32, own.shape, 0) < 4
        stats_ref[chip] = every + jnp.where(upper, own, other)
        stats_ref[chip + 1] = every + jnp.where(upper, other, own)

    ours, theirs = (row // 2 == core for core in (side, 1 - side))
    for step in range(4):
        for four in range(fours):
            at = step * fours + four
            chip = receiver(me, fours, step, four)
            first, second = first_ref[chip], second_ref[chip]
            turned_first = jnp.where(row % 4 < 2, pltpu.roll(first, 6, 0), pltpu.roll(first, 2, 0))
            lower = jnp.where(row < 4, 0.0, first)
            here, there = (near_ref, far_ref) if not crosses(fours, step, four) else (far_ref, near_ref)
            direct, swapped = (first, turned_first) if not crosses(fours, step, four) else (turned_first, first)
            here[0, at], here[1, at] = lower, second
            there[0, at] = there[1, at] = jnp.zeros_like(lower)
            near_ref[2, at] = jnp.where(ours, direct, 0.0)
            far_ref[2, at] = jnp.where(theirs, swapped, 0.0)

    total = None
    for ref, token_half, upstream_half in ((near_ref, tokens_ref, upstream_ref), (far_ref, tokens_far_ref, upstream_far_ref)):
        rows = ref[...].reshape(3 * 8 * seq, patches).astype(BF16)
        by_tokens = dot(rows[: 16 * seq], token_half[...])
        left, right = by_tokens[: 8 * seq] + dot(rows[16 * seq :], upstream_half[...]), by_tokens[8 * seq :]
        total = (left, right) if total is None else (total[0] + left, total[1] + right)
    left, right = (value.reshape(4, fours, 8, half).astype(BF16) for value in total)
    for step, send_ref in enumerate(sends):
        send_ref[:, :, :half] = left[step]
        send_ref[:, :, half : 2 * half] = right[step]
        for four in range(fours):
            send_ref[four, :, 2 * half :] = stats_ref[receiver(me, fours, step, four)].astype(BF16)


def column_stats(stats, groups):
    extra = stats.shape[1]
    pair = stats + pltpu.roll(stats, extra - groups, 1)
    return pair, pltpu.roll(pair, extra - 2 * groups, 1), pltpu.roll(pair, extra - 4 * groups, 1)


def merge_stats(chunks, half, groups):
    blocks = [column_stats(chunk[:, 2 * half :].astype(F32), groups) for chunk in chunks]
    high = functools.reduce(jnp.maximum, [top for top, _, _ in blocks])
    scales = [jnp.exp(top - high) for top, _, _ in blocks]
    total = sum(scale * value for scale, (_, value, _) in zip(scales, blocks))
    inner = sum(scale * value for scale, (_, _, value) in zip(scales, blocks))
    return high, total, inner, scales, [inner / total for _, total, inner in blocks]


def merge_kernel(*refs, groups, half):
    chunk_refs, out_ref = refs[:4], refs[4]
    fours, _, width = chunk_refs[0].shape
    merged = out_ref.shape[0]
    lane = lax.broadcasted_iota(jnp.int32, (8, width - 2 * half), 1)
    upper = lax.broadcasted_iota(jnp.int32, lane.shape, 0) < 4
    for four in range(merged):
        chunks = [ref.at[four + fours - merged] for ref in chunk_refs]
        high, total, inner, scales, means = merge_stats(chunks, half, groups)
        stats = [part for stat in (high, total, inner) for part in split16(stat)]
        centre = (stats[4] + stats[5]) / (stats[2] + stats[3])
        left = right = jnp.zeros((8, half), F32)
        for chunk, scale, mean in zip(chunks, scales, means):
            weight = jnp.where(upper, 1.0, scale)[:, 0:1]
            moved = jnp.where(upper, 0.0, scale * (mean - centre))[:, 0:1]
            by_right = chunk[:, half : 2 * half].astype(F32)
            left = left + weight * chunk[:, :half].astype(F32) + moved * by_right
            right = right + weight * by_right
        out_ref[four, :, :half] = left.astype(BF16)
        out_ref[four, :, half : 2 * half] = right.astype(BF16)
        block = sum(pltpu.roll(jnp.where(lane < groups, stat, 0.0), j * groups, 1) for j, stat in enumerate(stats))
        out_ref[four, :, 2 * half :] = block.astype(BF16)


def finish_kernel(*refs):
    inputs, outs_and_scratch = refs[:-8], refs[-8:]
    slots_ref, other_ref, col_ref, row_ref, disp_ref, mine_ref, *rest = inputs
    params_out, tokens_out, sums_out, rows_ref, params_ref, tokens_ref, sums_ref, sems = outs_and_scratch
    side = lax.axis_index("exp")
    half = params_ref.shape[1]
    seq = slots_ref.shape[0]
    n_slots = col_ref.shape[0]
    groups = n_slots // 8 + 1
    if seq == 8:
        chunks = [ref.at[0] for ref in (mine_ref, *rest)]
    else:
        chunks = [rest[0].at[four] for four in range(rest[0].shape[0])]
    high, total, inner, scales, means = merge_stats(chunks, half, groups)
    centre = inner / total

    top, _, _ = column_stats(mine_ref[0, :, 2 * half :].astype(F32), groups)
    weight = jnp.exp(top - high) / total
    zero = jnp.zeros((6, col_ref.shape[1]), F32)
    for group in range(groups - 1):
        span = slice(8 * group, 8 * group + 8)
        dispatch = col_ref[span] * weight[:, group + 1 : group + 2]
        d_logit = row_ref[span] + dispatch * (disp_ref[span] - centre[:, group + 1 : group + 2])
        first = jnp.where(side == 0, dispatch, pltpu.roll(dispatch, 6, 0))
        second = jnp.where(side == 0, pltpu.roll(dispatch, 6, 0), dispatch)
        for j in range(2):
            span = slice(16 * group + 8 * j, 16 * group + 8 * j + 8)
            ahead = lax.rem(owner(2 * group + j, seq) + side, 2)
            ours, theirs = first[4 * j : 4 * j + 2], second[4 * j : 4 * j + 2]
            rows_ref[ahead, span, :] = jnp.concatenate([d_logit[4 * j : 4 * j + 4], ours, zero[0:2]], axis=0)
            rows_ref[1 - ahead, span, :] = jnp.concatenate([zero, theirs], axis=0)
    left = rows_ref[...].reshape(16 * seq, -1).astype(BF16)
    right = jnp.concatenate([ref[:, :, :half].reshape(8 * seq, half) for ref in (slots_ref, other_ref)], axis=0)
    patches = tokens_ref.shape[0] // 2
    copies = []
    for part in range(2):
        span = slice(part * patches, (part + 1) * patches)
        tokens_ref[span, :] = dot_tn(left[:, span], right).astype(BF16)
        copies.append(pltpu.make_async_copy(tokens_ref.at[span], tokens_out.at[span], sems.at[part]))
        copies[-1].start()

    upper = lax.broadcasted_iota(jnp.int32, centre.shape, 0) < 4
    left = right = jnp.zeros((8, half), F32)
    for chunk, scale, mean in zip(chunks, scales, means):
        weight = scale / total
        by_left = jnp.where(upper, 1.0, weight)
        by_right = jnp.where(upper, 1.0, weight * (mean - centre))
        left = left + by_left[:, 0:1] * chunk[:, :half].astype(F32)
        right = right + by_right[:, 0:1] * chunk[:, half : 2 * half].astype(F32)
    sums_ref[:, :half] = left[0:2]
    sums_ref[:, half:] = left[2:4]
    params_ref[...] = left[4:8] + right[0:4] + right[4:8]
    for i, (source, target) in enumerate(((params_ref, params_out), (sums_ref, sums_out))):
        copies.append(pltpu.make_async_copy(source, target, sems.at[2 + i]))
        copies[-1].start()
    for copy in copies:
        copy.wait()


def to_other_core(value, seq, step):
    pairs = [(2 * chip + core, 2 * (chip ^ step) + 1 - core) for chip in range(seq) for core in range(2)]
    return lax.ppermute(value, ("seq", "exp"), pairs)


def shards(seq, tokens, upstream, slot_params, slot_outputs, slot_input_grads):
    patches, half = tokens.shape
    n_slots = slot_params.shape[0] * seq
    extra = -(-6 * (n_slots // 8 + 1) // 128) * 128
    sds = jax.ShapeDtypeStruct
    cores = [(0, 1), (1, 0)]

    tokens_far, far = (lax.ppermute(x, "exp", cores) for x in (tokens, upstream))
    seed = call(seed_kernel, sds((8, 128), F32), "seed", seq, cost_estimate=LONG)()
    fours = seq // 4
    rows = (8, half + half // 2)
    chunks = call(pack_kernel, sds((1 if fours == 2 else seq, *rows), BF16), "pack", seq)(
        seed, slot_params, slot_outputs, slot_input_grads
    )
    if fours == 2:
        taken = to_other_core(chunks, seq, 4)
        pieces = [call(pair_kernel, sds((2, *rows), BF16), "pair", seq)(chunks, taken)]
        pieces += [to_other_core(pieces[0], seq, step) for step in range(1, 4)]
        slots = call(order_kernel, sds((seq, *rows), BF16), "order", seq)(*pieces)
    else:
        slots = lax.all_to_all(chunks, "seq", split_axis=0, concat_axis=0, tiled=True)
    other = lax.ppermute(slots, "exp", cores)
    by_slot = sds((n_slots, patches), F32)
    turned = sds((half, patches), BF16)
    near = call(near_kernel, (turned,) * 4 + (by_slot,) * 3, "near", seq, cost_estimate=LONG)(
        slots, tokens, tokens_far, upstream, far
    )
    chunk = (8, 2 * half + extra)
    *sends, col, row, disp = call(
        local_kernel,
        (sds((fours, *chunk), BF16),) * 4 + (by_slot,) * 3,
        "local",
        seq,
        [pltpu.VMEM((seq, 8, patches), F32)] * 2
        + [pltpu.VMEM((seq, 8, extra), F32)]
        + [pltpu.VMEM((3, seq, 8, patches), F32)] * 2,
    )(other, tokens, tokens_far, upstream, far, *near)
    got = [sends[0]] + [to_other_core(sends[step], seq, step) for step in (3, 2, 1)]
    merged = call(
        functools.partial(merge_kernel, groups=n_slots // 8 + 1, half=half),
        sds((1 if fours == 2 else fours, *chunk), BF16),
        "merge",
        seq,
    )(*got)
    if fours == 2:
        got.append(to_other_core(merged, seq, 4))
    else:
        same = [[4 * four + step for four in range(fours)] for step in range(4)]
        got[1:] = [lax.all_to_all(merged, "seq", split_axis=0, concat_axis=0, tiled=True, axis_index_groups=same)]
    param_grads, token_grads, slot_output_grads = call(
        finish_kernel,
        (sds((4, half), F32), sds((patches, half), BF16), sds((2, 2 * half), F32)),
        "finish",
        seq,
        [
            pltpu.VMEM((2, 8 * seq, patches), F32),
            pltpu.VMEM((4, half), F32),
            pltpu.VMEM((patches, half), BF16),
            pltpu.VMEM((2, 2 * half), F32),
            pltpu.SemaphoreType.DMA((4,)),
        ],
        out_specs=[pl.BlockSpec(memory_space=pl.ANY)] * 3,
    )(slots, other, col, row, disp, *got)
    return token_grads, param_grads, slot_output_grads


def solution(mesh):
    in_specs = (
        P(("group", "seq"), "exp"),
        P(("group", "seq"), "exp"),
        P(("group", "seq"), "exp"),
        P(("group", "seq", "exp"), None),
        P(("group", "seq", "exp"), None),
    )
    out_specs = (
        P(("group", "seq"), "exp"),
        P(("group", "seq"), "exp"),
        P(("group", "seq", "exp"), None),
    )
    return jax.shard_map(
        functools.partial(shards, mesh.shape["seq"]),
        mesh=mesh,
        in_specs=in_specs,
        out_specs=out_specs,
        check_vma=False,
    )
```

```python
import functools

import jax
import jax.numpy as jnp
from jax import lax
from jax.experimental import pallas as pl
from jax.experimental.pallas import tpu as pltpu
from jax.sharding import PartitionSpec as P

F32 = jnp.float32
BF16 = jnp.bfloat16
LONG = pl.CostEstimate(flops=10**10, bytes_accessed=10**7, transcendentals=0)


def dot(left, right):
    return jnp.dot(left, right, preferred_element_type=F32)


def dot_tn(left, right):
    return lax.dot_general(left, right, (((0,), (0,)), ((), ())), preferred_element_type=F32)


def call(kernel, outs, name, seq, scratch=(), **specs):
    return pl.pallas_call(
        kernel,
        out_shape=outs,
        scratch_shapes=list(scratch),
        compiler_params=pltpu.CompilerParams(vmem_limit_bytes=(16 if seq <= 16 else 48) << 20),
        name=name,
        **specs,
    )


def split16(value):
    high = value.astype(BF16).astype(F32)
    return high, (value - high).astype(BF16).astype(F32)


def receiver(me, fours, step, four):
    return lax.bitwise_xor(me, step + 4 * four) if fours == 2 else 4 * four + lax.bitwise_xor(lax.rem(me, 4), step)


def crosses(fours, step, four):
    return (step > 0) != (fours == 2 and four > 0)


def seed_kernel(seed_ref):
    seed_ref[...] = jnp.zeros_like(seed_ref)


def pack_kernel(seed_ref, params_ref, outs_ref, grads_ref, chunks_ref):
    side = lax.axis_index("exp")
    half = params_ref.shape[1]
    quarter = half // 2

    def halves(ref):
        value = ref[...].astype(F32)
        first, second = value[:, :half], value[:, half:]
        return jnp.where(side == 0, first, second), jnp.where(side == 0, second, first)

    own, far = halves(outs_ref)
    pieces = (own[:, :quarter], own[:, quarter:], far[:, :quarter], far[:, quarter:])
    left = jnp.concatenate([params_ref[...].astype(F32), *halves(grads_ref)], axis=0).astype(BF16)
    right = jnp.concatenate(pieces, axis=0).astype(BF16)
    for dest in range(chunks_ref.shape[0]):
        chunks_ref[dest, :, :half] = left
        chunks_ref[dest, :, half:] = right


def pair_kernel(mine_ref, taken_ref, pair_ref):
    pair_ref[0:1] = mine_ref[...]
    pair_ref[1:2] = taken_ref[...]


def order_kernel(*refs):
    me = lax.axis_index("seq")
    *piece_refs, slots_ref = refs
    for step, piece_ref in enumerate(piece_refs):
        for four in range(2):
            slots_ref[receiver(me, 2, step, four)] = piece_ref[four]


def owner(chip, seq):
    side = lax.axis_index("exp")
    if seq != 8:
        return side
    path = lax.bitwise_xor(chip, lax.axis_index("seq"))
    return lax.rem(side + (lax.rem(path, 4) > 0).astype(jnp.int32) + path // 4, 2)


def products(slots_ref, tokens_ref, tokens_far_ref, upstream_ref, upstream_far_ref, cores):
    side = lax.axis_index("exp")
    seq, _, width = slots_ref.shape
    half = tokens_ref.shape[0]
    quarter = half // 2
    left = slots_ref[:, :, :half].reshape(8 * seq, half)
    right = slots_ref[:, :, half:].reshape(8 * seq, quarter)
    near, far = dot(left, tokens_ref[...]), dot(left, tokens_far_ref[...])
    by_quarter = [
        dot(right, ref[i * quarter : (i + 1) * quarter, :])
        for ref in (upstream_ref, upstream_far_ref)
        for i in range(2)
    ]
    row = lax.broadcasted_iota(jnp.int32, (8, near.shape[1]), 0)
    blocks = []
    for chip in range(0, seq, 2):
        parts = []
        for core, at in ((cores[chip], 8 * chip), (cores[chip + 1], 8 * chip + 8)):
            direct = core == side
            one, two, three, four, same, cross = (block[at : at + 8] for block in (*by_quarter, near, far))
            one, three = jnp.where(direct, one, three), jnp.where(direct, three, one)
            two, four = jnp.where(direct, two, four), jnp.where(direct, four, two)
            same, cross = jnp.where(direct, same, cross), jnp.where(direct, cross, same)
            comb = jnp.where(row < 4, jnp.where(row < 2, one, two), jnp.where(row < 6, three, four))
            disp = jnp.where(row < 4, 0.0, jnp.where(row < 6, same, cross))
            comb, disp = comb + pltpu.roll(comb, 4, 0), disp + pltpu.roll(disp, 4, 0)
            comb, disp = comb + pltpu.roll(comb, 2, 0), disp + pltpu.roll(disp, 2, 0)
            ours = row // 2 % 2 == core
            parts.append((same, jnp.where(ours, comb, 0.0), jnp.where(ours, disp, 0.0)))
        (even, even_comb, even_disp), (odd, odd_comb, odd_disp) = parts
        logits = jnp.where(row < 4, even, pltpu.roll(odd, 4, 0))
        blocks.append((logits, jnp.where(row < 4, even_comb, odd_comb), jnp.where(row < 4, even_disp, odd_disp)))
    return [jnp.concatenate(parts, axis=0) for parts in zip(*blocks)]


def near_kernel(slots_ref, *refs):
    inputs, turned, part_refs = refs[:4], refs[4:8], refs[8:]
    seq = slots_ref.shape[0]
    for source, target in zip(inputs, turned):
        target[...] = source[...].T
    cores = [owner(chip, seq) for chip in range(seq)]
    for ref, part in zip(part_refs, products(slots_ref, *turned, cores)):
        ref[...] = part


def local_kernel(
    slots_ref, tokens_ref, tokens_far_ref, upstream_ref, upstream_far_ref, *refs
):
    turned, (logit_ref, comb_ref, disp_ref), outs = refs[:4], refs[4:7], refs[7:]
    sends = [ref.at[place] for ref in outs[:-8] for place in range(ref.shape[0])]
    col_ref, row_ref, d_disp_ref, first_ref, second_ref, stats_ref, near_ref, far_ref = outs[-8:]
    side, me = lax.axis_index("exp"), lax.axis_index("seq")
    n_slots, patches = col_ref.shape
    seq = n_slots // 4
    fours = seq // 4
    half = tokens_ref.shape[1]
    extra = stats_ref.shape[2]
    groups = n_slots // 8 + 1
    parts = products(slots_ref, *turned, [1 - owner(chip, seq) for chip in range(seq)])
    logits, d_comb, d_disp = (ref[...] + part for ref, part in zip((logit_ref, comb_ref, disp_ref), parts))
    row_exp = jnp.exp(logits - jnp.max(logits, axis=0, keepdims=True))
    combine = row_exp / jnp.sum(row_exp, axis=0, keepdims=True)
    row_part = combine * (d_comb - jnp.sum(combine * d_comb, axis=0, keepdims=True))
    top_high, top_low = split16(jnp.max(logits, axis=1, keepdims=True))
    col_exp = jnp.exp(logits - (top_high + top_low))
    sum_high, sum_low = split16(jnp.sum(col_exp, axis=1, keepdims=True))
    inner_high, inner_low = split16(jnp.sum(col_exp * d_disp, axis=1, keepdims=True))
    centre = (inner_high + inner_low) / (sum_high + sum_low)
    col_part = col_exp * (d_disp - centre)
    col_ref[...] = col_exp
    row_ref[...] = row_part
    d_disp_ref[...] = d_disp

    lane = lax.broadcasted_iota(jnp.int32, (n_slots, extra), 1)
    stats = jnp.zeros((n_slots, extra), F32)
    for j, stat in enumerate((top_high, top_low, sum_high, sum_low, inner_high, inner_low)):
        stats = jnp.where(lane == j * groups, stat, stats)
    every = jnp.zeros((8, extra), F32)
    for group in range(groups - 1):
        every = every + pltpu.roll(stats[8 * group : 8 * group + 8], group + 1, 1)

    row = lax.broadcasted_iota(jnp.int32, (8, patches), 0)
    for chip in range(0, seq, 2):
        span = slice(4 * chip, 4 * chip + 8)
        for ref, upper, lower in ((first_ref, combine, col_part), (second_ref, row_part, col_exp)):
            upper, lower = upper[span], lower[span]
            ref[chip] = jnp.where(row < 4, upper, pltpu.roll(lower, 4, 0))
            ref[chip + 1] = jnp.where(row < 4, pltpu.roll(upper, 4, 0), lower)
        own = stats[span]
        other = pltpu.roll(own, 4, 0)
        upper = lax.broadcasted_iota(jnp.int32, own.shape, 0) < 4
        stats_ref[chip] = every + jnp.where(upper, own, other)
        stats_ref[chip + 1] = every + jnp.where(upper, other, own)

    ours, theirs = (row // 2 == core for core in (side, 1 - side))
    for step in range(4):
        for four in range(fours):
            at = step * fours + four
            chip = receiver(me, fours, step, four)
            first, second = first_ref[chip], second_ref[chip]
            turned_first = jnp.where(row % 4 < 2, pltpu.roll(first, 6, 0), pltpu.roll(first, 2, 0))
            lower = jnp.where(row < 4, 0.0, first)
            here, there = (near_ref, far_ref) if not crosses(fours, step, four) else (far_ref, near_ref)
            direct, swapped = (first, turned_first) if not crosses(fours, step, four) else (turned_first, first)
            here[0, at], here[1, at] = lower, second
            there[0, at] = there[1, at] = jnp.zeros_like(lower)
            near_ref[2, at] = jnp.where(ours, direct, 0.0)
            far_ref[2, at] = jnp.where(theirs, swapped, 0.0)

    total = None
    for ref, token_half, upstream_half in ((near_ref, tokens_ref, upstream_ref), (far_ref, tokens_far_ref, upstream_far_ref)):
        rows = ref[...].reshape(3 * 8 * seq, patches).astype(BF16)
        by_tokens = dot(rows[: 16 * seq], token_half[...])
        left, right = by_tokens[: 8 * seq] + dot(rows[16 * seq :], upstream_half[...]), by_tokens[8 * seq :]
        total = (left, right) if total is None else (total[0] + left, total[1] + right)
    left, right = (value.reshape(seq, 8, half).astype(BF16) for value in total)
    for at, send_ref in enumerate(sends):
        send_ref[:, :half] = left[at]
        send_ref[:, half : 2 * half] = right[at]
        send_ref[:, 2 * half :] = stats_ref[receiver(me, fours, at // fours, at % fours)].astype(BF16)


def column_stats(stats, groups):
    extra = stats.shape[1]
    pair = stats + pltpu.roll(stats, extra - groups, 1)
    return pair, pltpu.roll(pair, extra - 2 * groups, 1), pltpu.roll(pair, extra - 4 * groups, 1)


def merge_stats(chunks, half, groups):
    blocks = [column_stats(chunk[:, 2 * half :].astype(F32), groups) for chunk in chunks]
    high = functools.reduce(jnp.maximum, [top for top, _, _ in blocks])
    scales = [jnp.exp(top - high) for top, _, _ in blocks]
    total = sum(scale * value for scale, (_, value, _) in zip(scales, blocks))
    inner = sum(scale * value for scale, (_, _, value) in zip(scales, blocks))
    return high, total, inner, scales, [inner / total for _, total, inner in blocks]


def merge_kernel(*refs, groups, half):
    chunk_refs, out_ref = refs[:4], refs[4]
    merged, _, width = out_ref.shape
    lane = lax.broadcasted_iota(jnp.int32, (8, width - 2 * half), 1)
    upper = lax.broadcasted_iota(jnp.int32, lane.shape, 0) < 4
    for four in range(merged):
        chunks = [ref.at[four] for ref in chunk_refs]
        high, total, inner, scales, means = merge_stats(chunks, half, groups)
        stats = [part for stat in (high, total, inner) for part in split16(stat)]
        centre = (stats[4] + stats[5]) / (stats[2] + stats[3])
        left = right = jnp.zeros((8, half), F32)
        for chunk, scale, mean in zip(chunks, scales, means):
            weight = jnp.where(upper, 1.0, scale)[:, 0:1]
            moved = jnp.where(upper, 0.0, scale * (mean - centre))[:, 0:1]
            by_right = chunk[:, half : 2 * half].astype(F32)
            left = left + weight * chunk[:, :half].astype(F32) + moved * by_right
            right = right + weight * by_right
        out_ref[four, :, :half] = left.astype(BF16)
        out_ref[four, :, half : 2 * half] = right.astype(BF16)
        block = sum(pltpu.roll(jnp.where(lane < groups, stat, 0.0), j * groups, 1) for j, stat in enumerate(stats))
        out_ref[four, :, 2 * half :] = block.astype(BF16)


def finish_kernel(*refs):
    inputs, outs_and_scratch = refs[:-8], refs[-8:]
    slots_ref, other_ref, col_ref, row_ref, disp_ref, mine_ref, *rest = inputs
    params_out, tokens_out, sums_out, rows_ref, params_ref, tokens_ref, sums_ref, sems = outs_and_scratch
    side = lax.axis_index("exp")
    half = params_ref.shape[1]
    seq = slots_ref.shape[0]
    n_slots = col_ref.shape[0]
    groups = n_slots // 8 + 1
    if seq == 8:
        chunks = [ref.at[0] for ref in (mine_ref, *rest)]
    else:
        chunks = [rest[0].at[four] for four in range(rest[0].shape[0])]
    high, total, inner, scales, means = merge_stats(chunks, half, groups)
    centre = inner / total

    top, _, _ = column_stats(mine_ref[0, :, 2 * half :].astype(F32), groups)
    weight = jnp.exp(top - high) / total
    zero = jnp.zeros((6, col_ref.shape[1]), F32)
    for group in range(groups - 1):
        span = slice(8 * group, 8 * group + 8)
        dispatch = col_ref[span] * weight[:, group + 1 : group + 2]
        d_logit = row_ref[span] + dispatch * (disp_ref[span] - centre[:, group + 1 : group + 2])
        first = jnp.where(side == 0, dispatch, pltpu.roll(dispatch, 6, 0))
        second = jnp.where(side == 0, pltpu.roll(dispatch, 6, 0), dispatch)
        for j in range(2):
            span = slice(16 * group + 8 * j, 16 * group + 8 * j + 8)
            ahead = lax.rem(owner(2 * group + j, seq) + side, 2)
            ours, theirs = first[4 * j : 4 * j + 2], second[4 * j : 4 * j + 2]
            rows_ref[ahead, span, :] = jnp.concatenate([d_logit[4 * j : 4 * j + 4], ours, zero[0:2]], axis=0)
            rows_ref[1 - ahead, span, :] = jnp.concatenate([zero, theirs], axis=0)
    left = rows_ref[...].reshape(16 * seq, -1).astype(BF16)
    right = jnp.concatenate([ref[:, :, :half].reshape(8 * seq, half) for ref in (slots_ref, other_ref)], axis=0)
    patches = tokens_ref.shape[0] // 2
    copies = []
    for part in range(2):
        span = slice(part * patches, (part + 1) * patches)
        tokens_ref[span, :] = dot_tn(left[:, span], right).astype(BF16)
        copies.append(pltpu.make_async_copy(tokens_ref.at[span], tokens_out.at[span], sems.at[part]))
        copies[-1].start()

    upper = lax.broadcasted_iota(jnp.int32, centre.shape, 0) < 4
    left = right = jnp.zeros((8, half), F32)
    for chunk, scale, mean in zip(chunks, scales, means):
        weight = scale / total
        by_left = jnp.where(upper, 1.0, weight)
        by_right = jnp.where(upper, 1.0, weight * (mean - centre))
        left = left + by_left[:, 0:1] * chunk[:, :half].astype(F32)
        right = right + by_right[:, 0:1] * chunk[:, half : 2 * half].astype(F32)
    sums_ref[:, :half] = left[0:2]
    sums_ref[:, half:] = left[2:4]
    params_ref[...] = left[4:8] + right[0:4] + right[4:8]
    for i, (source, target) in enumerate(((params_ref, params_out), (sums_ref, sums_out))):
        copies.append(pltpu.make_async_copy(source, target, sems.at[2 + i]))
        copies[-1].start()
    for copy in copies:
        copy.wait()


def to_other_core(value, seq, step):
    pairs = [(2 * chip + core, 2 * (chip ^ step) + 1 - core) for chip in range(seq) for core in range(2)]
    return lax.ppermute(value, ("seq", "exp"), pairs)


def shards(seq, tokens, upstream, slot_params, slot_outputs, slot_input_grads):
    patches, half = tokens.shape
    n_slots = slot_params.shape[0] * seq
    extra = -(-6 * (n_slots // 8 + 1) // 128) * 128
    sds = jax.ShapeDtypeStruct
    cores = [(0, 1), (1, 0)]

    tokens_far, far = (lax.ppermute(x, "exp", cores) for x in (tokens, upstream))
    seed = call(seed_kernel, sds((8, 128), F32), "seed", seq, cost_estimate=LONG)()
    fours = seq // 4
    rows = (8, half + half // 2)
    chunks = call(pack_kernel, sds((1 if fours == 2 else seq, *rows), BF16), "pack", seq)(
        seed, slot_params, slot_outputs, slot_input_grads
    )
    if fours == 2:
        taken = to_other_core(chunks, seq, 4)
        pieces = [call(pair_kernel, sds((2, *rows), BF16), "pair", seq)(chunks, taken)]
        pieces += [to_other_core(pieces[0], seq, step) for step in range(1, 4)]
        slots = call(order_kernel, sds((seq, *rows), BF16), "order", seq)(*pieces)
    else:
        slots = lax.all_to_all(chunks, "seq", split_axis=0, concat_axis=0, tiled=True)
    other = lax.ppermute(slots, "exp", cores)
    by_slot = sds((n_slots, patches), F32)
    turned = sds((half, patches), BF16)
    near = call(near_kernel, (turned,) * 4 + (by_slot,) * 3, "near", seq, cost_estimate=LONG)(
        slots, tokens, tokens_far, upstream, far
    )
    chunk = (8, 2 * half + extra)
    parts = 2 if fours == 2 else 1
    *sends, col, row, disp = call(
        local_kernel,
        (sds((fours // parts, *chunk), BF16),) * (4 * parts) + (by_slot,) * 3,
        "local",
        seq,
        [pltpu.VMEM((seq, 8, patches), F32)] * 2
        + [pltpu.VMEM((seq, 8, extra), F32)]
        + [pltpu.VMEM((3, seq, 8, patches), F32)] * 2,
    )(other, tokens, tokens_far, upstream, far, *near)
    theirs = [to_other_core(sends[parts * step + parts - 1], seq, step) for step in (3, 2, 1)]
    ours = [to_other_core(sends[parts * step], seq, step) for step in (3, 2, 1)] if fours == 2 else []
    merged = call(
        functools.partial(merge_kernel, groups=n_slots // 8 + 1, half=half),
        sds((fours // parts, *chunk), BF16),
        "merge",
        seq,
    )(sends[parts - 1], *theirs)
    if fours == 2:
        got = [to_other_core(merged, seq, 4), *ours]
    else:
        same = [[4 * four + step for four in range(fours)] for step in range(4)]
        got = [lax.all_to_all(merged, "seq", split_axis=0, concat_axis=0, tiled=True, axis_index_groups=same)]
    param_grads, token_grads, slot_output_grads = call(
        finish_kernel,
        (sds((4, half), F32), sds((patches, half), BF16), sds((2, 2 * half), F32)),
        "finish",
        seq,
        [
            pltpu.VMEM((2, 8 * seq, patches), F32),
            pltpu.VMEM((4, half), F32),
            pltpu.VMEM((patches, half), BF16),
            pltpu.VMEM((2, 2 * half), F32),
            pltpu.SemaphoreType.DMA((4,)),
        ],
        out_specs=[pl.BlockSpec(memory_space=pl.ANY)] * 3,
    )(slots, other, col, row, disp, sends[0], *got)
    return token_grads, param_grads, slot_output_grads


def solution(mesh):
    in_specs = (
        P(("group", "seq"), "exp"),
        P(("group", "seq"), "exp"),
        P(("group", "seq"), "exp"),
        P(("group", "seq", "exp"), None),
        P(("group", "seq", "exp"), None),
    )
    out_specs = (
        P(("group", "seq"), "exp"),
        P(("group", "seq"), "exp"),
        P(("group", "seq", "exp"), None),
    )
    return jax.shard_map(
        functools.partial(shards, mesh.shape["seq"]),
        mesh=mesh,
        in_specs=in_specs,
        out_specs=out_specs,
        check_vma=False,
    )
```

```python
import functools

import jax
import jax.numpy as jnp
from jax import lax
from jax.experimental import pallas as pl
from jax.experimental.pallas import tpu as pltpu
from jax.sharding import PartitionSpec as P

F32 = jnp.float32
BF16 = jnp.bfloat16
LONG = pl.CostEstimate(flops=10**10, bytes_accessed=10**7, transcendentals=0)


def dot(left, right):
    return jnp.dot(left, right, preferred_element_type=F32)


def dot_tn(left, right):
    return lax.dot_general(left, right, (((0,), (0,)), ((), ())), preferred_element_type=F32)


def call(kernel, outs, name, seq, scratch=(), **specs):
    return pl.pallas_call(
        kernel,
        out_shape=outs,
        scratch_shapes=list(scratch),
        compiler_params=pltpu.CompilerParams(vmem_limit_bytes=(16 if seq <= 16 else 48) << 20),
        name=name,
        **specs,
    )


def split16(value):
    high = value.astype(BF16).astype(F32)
    return high, (value - high).astype(BF16).astype(F32)


def receiver(me, fours, step, four):
    return lax.bitwise_xor(me, step + 4 * four) if fours == 2 else 4 * four + lax.bitwise_xor(lax.rem(me, 4), step)


def crosses(fours, step, four):
    return (step > 0) != (fours == 2 and four > 0)


def seed_kernel(seed_ref):
    seed_ref[...] = jnp.zeros_like(seed_ref)


def pack_kernel(seed_ref, params_ref, outs_ref, grads_ref, chunks_ref):
    side = lax.axis_index("exp")
    half = params_ref.shape[1]
    quarter = half // 2

    def halves(ref):
        value = ref[...].astype(F32)
        first, second = value[:, :half], value[:, half:]
        return jnp.where(side == 0, first, second), jnp.where(side == 0, second, first)

    own, far = halves(outs_ref)
    pieces = (own[:, :quarter], own[:, quarter:], far[:, :quarter], far[:, quarter:])
    left = jnp.concatenate([params_ref[...].astype(F32), *halves(grads_ref)], axis=0).astype(BF16)
    right = jnp.concatenate(pieces, axis=0).astype(BF16)
    for dest in range(chunks_ref.shape[0]):
        chunks_ref[dest, :, :half] = left
        chunks_ref[dest, :, half:] = right


def pair_kernel(mine_ref, taken_ref, pair_ref):
    pair_ref[0:1] = mine_ref[...]
    pair_ref[1:2] = taken_ref[...]


def order_kernel(*refs):
    me = lax.axis_index("seq")
    *piece_refs, slots_ref = refs
    for step, piece_ref in enumerate(piece_refs):
        for four in range(2):
            slots_ref[receiver(me, 2, step, four)] = piece_ref[four]


def owner(chip, seq):
    side = lax.axis_index("exp")
    if seq != 8:
        return side
    path = lax.bitwise_xor(chip, lax.axis_index("seq"))
    return lax.rem(side + (lax.rem(path, 4) > 0).astype(jnp.int32) + path // 4, 2)


def products(slots_ref, tokens_ref, tokens_far_ref, upstream_ref, upstream_far_ref, cores):
    side = lax.axis_index("exp")
    seq, _, width = slots_ref.shape
    half = tokens_ref.shape[0]
    quarter = half // 2
    left = slots_ref[:, :, :half].reshape(8 * seq, half)
    right = slots_ref[:, :, half:].reshape(8 * seq, quarter)
    near, far = dot(left, tokens_ref[...]), dot(left, tokens_far_ref[...])
    by_quarter = [
        dot(right, ref[i * quarter : (i + 1) * quarter, :])
        for ref in (upstream_ref, upstream_far_ref)
        for i in range(2)
    ]
    row = lax.broadcasted_iota(jnp.int32, (8, near.shape[1]), 0)
    blocks = []
    for chip in range(0, seq, 2):
        parts = []
        for core, at in ((cores[chip], 8 * chip), (cores[chip + 1], 8 * chip + 8)):
            direct = core == side
            one, two, three, four, same, cross = (block[at : at + 8] for block in (*by_quarter, near, far))
            one, three = jnp.where(direct, one, three), jnp.where(direct, three, one)
            two, four = jnp.where(direct, two, four), jnp.where(direct, four, two)
            same, cross = jnp.where(direct, same, cross), jnp.where(direct, cross, same)
            comb = jnp.where(row < 4, jnp.where(row < 2, one, two), jnp.where(row < 6, three, four))
            disp = jnp.where(row < 4, 0.0, jnp.where(row < 6, same, cross))
            comb, disp = comb + pltpu.roll(comb, 4, 0), disp + pltpu.roll(disp, 4, 0)
            comb, disp = comb + pltpu.roll(comb, 2, 0), disp + pltpu.roll(disp, 2, 0)
            ours = row // 2 % 2 == core
            parts.append((same, jnp.where(ours, comb, 0.0), jnp.where(ours, disp, 0.0)))
        (even, even_comb, even_disp), (odd, odd_comb, odd_disp) = parts
        logits = jnp.where(row < 4, even, pltpu.roll(odd, 4, 0))
        blocks.append((logits, jnp.where(row < 4, even_comb, odd_comb), jnp.where(row < 4, even_disp, odd_disp)))
    return [jnp.concatenate(parts, axis=0) for parts in zip(*blocks)]


def near_kernel(slots_ref, *refs):
    inputs, turned, part_refs = refs[:4], refs[4:8], refs[8:]
    seq = slots_ref.shape[0]
    for source, target in zip(inputs, turned):
        target[...] = source[...].T
    cores = [owner(chip, seq) for chip in range(seq)]
    for ref, part in zip(part_refs, products(slots_ref, *turned, cores)):
        ref[...] = part


def local_kernel(
    slots_ref, tokens_ref, tokens_far_ref, upstream_ref, upstream_far_ref, *refs
):
    turned, (logit_ref, comb_ref, disp_ref), outs = refs[:4], refs[4:7], refs[7:]
    sends = [ref.at[place] for ref in outs[:-8] for place in range(ref.shape[0])]
    col_ref, row_ref, d_disp_ref, first_ref, second_ref, stats_ref, near_ref, far_ref = outs[-8:]
    side, me = lax.axis_index("exp"), lax.axis_index("seq")
    n_slots, patches = col_ref.shape
    seq = n_slots // 4
    fours = seq // 4
    half = tokens_ref.shape[1]
    extra = stats_ref.shape[2]
    groups = n_slots // 8 + 1
    parts = products(slots_ref, *turned, [1 - owner(chip, seq) for chip in range(seq)])
    logits, d_comb, d_disp = (ref[...] + part for ref, part in zip((logit_ref, comb_ref, disp_ref), parts))
    row_exp = jnp.exp(logits - jnp.max(logits, axis=0, keepdims=True))
    combine = row_exp / jnp.sum(row_exp, axis=0, keepdims=True)
    row_part = combine * (d_comb - jnp.sum(combine * d_comb, axis=0, keepdims=True))
    top_high, top_low = split16(jnp.max(logits, axis=1, keepdims=True))
    col_exp = jnp.exp(logits - (top_high + top_low))
    sum_high, sum_low = split16(jnp.sum(col_exp, axis=1, keepdims=True))
    inner_high, inner_low = split16(jnp.sum(col_exp * d_disp, axis=1, keepdims=True))
    centre = (inner_high + inner_low) / (sum_high + sum_low)
    col_part = col_exp * (d_disp - centre)
    col_ref[...] = col_exp
    row_ref[...] = row_part
    d_disp_ref[...] = d_disp

    lane = lax.broadcasted_iota(jnp.int32, (n_slots, extra), 1)
    stats = jnp.zeros((n_slots, extra), F32)
    for j, stat in enumerate((top_high, top_low, sum_high, sum_low, inner_high, inner_low)):
        stats = jnp.where(lane == j * groups, stat, stats)
    every = jnp.zeros((8, extra), F32)
    for group in range(groups - 1):
        every = every + pltpu.roll(stats[8 * group : 8 * group + 8], group + 1, 1)

    row = lax.broadcasted_iota(jnp.int32, (8, patches), 0)
    for chip in range(0, seq, 2):
        span = slice(4 * chip, 4 * chip + 8)
        for ref, upper, lower in ((first_ref, combine, col_part), (second_ref, row_part, col_exp)):
            upper, lower = upper[span], lower[span]
            ref[chip] = jnp.where(row < 4, upper, pltpu.roll(lower, 4, 0))
            ref[chip + 1] = jnp.where(row < 4, pltpu.roll(upper, 4, 0), lower)
        own = stats[span]
        other = pltpu.roll(own, 4, 0)
        upper = lax.broadcasted_iota(jnp.int32, own.shape, 0) < 4
        stats_ref[chip] = every + jnp.where(upper, own, other)
        stats_ref[chip + 1] = every + jnp.where(upper, other, own)

    ours, theirs = (row // 2 == core for core in (side, 1 - side))
    for step in range(4):
        for four in range(fours):
            at = step * fours + four
            chip = receiver(me, fours, step, four)
            first, second = first_ref[chip], second_ref[chip]
            turned_first = jnp.where(row % 4 < 2, pltpu.roll(first, 6, 0), pltpu.roll(first, 2, 0))
            lower = jnp.where(row < 4, 0.0, first)
            here, there = (near_ref, far_ref) if not crosses(fours, step, four) else (far_ref, near_ref)
            direct, swapped = (first, turned_first) if not crosses(fours, step, four) else (turned_first, first)
            here[0, at], here[1, at] = lower, second
            there[0, at] = there[1, at] = jnp.zeros_like(lower)
            near_ref[2, at] = jnp.where(ours, direct, 0.0)
            far_ref[2, at] = jnp.where(theirs, swapped, 0.0)

    total = None
    for ref, token_half, upstream_half in ((near_ref, tokens_ref, upstream_ref), (far_ref, tokens_far_ref, upstream_far_ref)):
        rows = ref[...].reshape(3 * 8 * seq, patches).astype(BF16)
        by_tokens = dot(rows[: 16 * seq], token_half[...])
        left, right = by_tokens[: 8 * seq] + dot(rows[16 * seq :], upstream_half[...]), by_tokens[8 * seq :]
        total = (left, right) if total is None else (total[0] + left, total[1] + right)
    left, right = (value.reshape(seq, 8, half).astype(BF16) for value in total)
    for at, send_ref in enumerate(sends):
        send_ref[:, :half] = left[at]
        send_ref[:, half : 2 * half] = right[at]
        send_ref[:, 2 * half :] = stats_ref[receiver(me, fours, at // fours, at % fours)].astype(BF16)


def column_stats(stats, groups):
    extra = stats.shape[1]
    pair = stats + pltpu.roll(stats, extra - groups, 1)
    return pair, pltpu.roll(pair, extra - 2 * groups, 1), pltpu.roll(pair, extra - 4 * groups, 1)


def merge_stats(chunks, half, groups):
    blocks = [column_stats(chunk[:, 2 * half :].astype(F32), groups) for chunk in chunks]
    high = functools.reduce(jnp.maximum, [top for top, _, _ in blocks])
    scales = [jnp.exp(top - high) for top, _, _ in blocks]
    total = sum(scale * value for scale, (_, value, _) in zip(scales, blocks))
    inner = sum(scale * value for scale, (_, _, value) in zip(scales, blocks))
    return high, total, inner, scales, [inner / total for _, total, inner in blocks]


def merge_kernel(*refs, groups, half):
    chunk_refs, out_ref = refs[:4], refs[4]
    merged, _, width = out_ref.shape
    lane = lax.broadcasted_iota(jnp.int32, (8, width - 2 * half), 1)
    upper = lax.broadcasted_iota(jnp.int32, lane.shape, 0) < 4
    for four in range(merged):
        chunks = [ref.at[ref.shape[0] - merged + four] for ref in chunk_refs]
        high, total, inner, scales, means = merge_stats(chunks, half, groups)
        stats = [part for stat in (high, total, inner) for part in split16(stat)]
        centre = (stats[4] + stats[5]) / (stats[2] + stats[3])
        left = right = jnp.zeros((8, half), F32)
        for chunk, scale, mean in zip(chunks, scales, means):
            weight = jnp.where(upper, 1.0, scale)[:, 0:1]
            moved = jnp.where(upper, 0.0, scale * (mean - centre))[:, 0:1]
            by_right = chunk[:, half : 2 * half].astype(F32)
            left = left + weight * chunk[:, :half].astype(F32) + moved * by_right
            right = right + weight * by_right
        out_ref[four, :, :half] = left.astype(BF16)
        out_ref[four, :, half : 2 * half] = right.astype(BF16)
        block = sum(pltpu.roll(jnp.where(lane < groups, stat, 0.0), j * groups, 1) for j, stat in enumerate(stats))
        out_ref[four, :, 2 * half :] = block.astype(BF16)


def finish_kernel(*refs):
    inputs, outs_and_scratch = refs[:-8], refs[-8:]
    slots_ref, other_ref, col_ref, row_ref, disp_ref, mine_ref, *rest = inputs
    params_out, tokens_out, sums_out, rows_ref, params_ref, tokens_ref, sums_ref, sems = outs_and_scratch
    side = lax.axis_index("exp")
    half = params_ref.shape[1]
    seq = slots_ref.shape[0]
    n_slots = col_ref.shape[0]
    groups = n_slots // 8 + 1
    if seq == 8:
        chunks = [ref.at[0] for ref in (mine_ref, *rest)]
    else:
        chunks = [rest[0].at[four] for four in range(rest[0].shape[0])]
    high, total, inner, scales, means = merge_stats(chunks, half, groups)
    centre = inner / total

    top, _, _ = column_stats(mine_ref[0, :, 2 * half :].astype(F32), groups)
    weight = jnp.exp(top - high) / total
    zero = jnp.zeros((6, col_ref.shape[1]), F32)
    for group in range(groups - 1):
        span = slice(8 * group, 8 * group + 8)
        dispatch = col_ref[span] * weight[:, group + 1 : group + 2]
        d_logit = row_ref[span] + dispatch * (disp_ref[span] - centre[:, group + 1 : group + 2])
        first = jnp.where(side == 0, dispatch, pltpu.roll(dispatch, 6, 0))
        second = jnp.where(side == 0, pltpu.roll(dispatch, 6, 0), dispatch)
        for j in range(2):
            span = slice(16 * group + 8 * j, 16 * group + 8 * j + 8)
            ahead = lax.rem(owner(2 * group + j, seq) + side, 2)
            ours, theirs = first[4 * j : 4 * j + 2], second[4 * j : 4 * j + 2]
            rows_ref[ahead, span, :] = jnp.concatenate([d_logit[4 * j : 4 * j + 4], ours, zero[0:2]], axis=0)
            rows_ref[1 - ahead, span, :] = jnp.concatenate([zero, theirs], axis=0)
    left = rows_ref[...].reshape(16 * seq, -1).astype(BF16)
    right = jnp.concatenate([ref[:, :, :half].reshape(8 * seq, half) for ref in (slots_ref, other_ref)], axis=0)
    patches = tokens_ref.shape[0] // 2
    copies = []
    for part in range(2):
        span = slice(part * patches, (part + 1) * patches)
        tokens_ref[span, :] = dot_tn(left[:, span], right).astype(BF16)
        copies.append(pltpu.make_async_copy(tokens_ref.at[span], tokens_out.at[span], sems.at[part]))
        copies[-1].start()

    upper = lax.broadcasted_iota(jnp.int32, centre.shape, 0) < 4
    left = right = jnp.zeros((8, half), F32)
    for chunk, scale, mean in zip(chunks, scales, means):
        weight = scale / total
        by_left = jnp.where(upper, 1.0, weight)
        by_right = jnp.where(upper, 1.0, weight * (mean - centre))
        left = left + by_left[:, 0:1] * chunk[:, :half].astype(F32)
        right = right + by_right[:, 0:1] * chunk[:, half : 2 * half].astype(F32)
    sums_ref[:, :half] = left[0:2]
    sums_ref[:, half:] = left[2:4]
    params_ref[...] = left[4:8] + right[0:4] + right[4:8]
    for i, (source, target) in enumerate(((params_ref, params_out), (sums_ref, sums_out))):
        copies.append(pltpu.make_async_copy(source, target, sems.at[2 + i]))
        copies[-1].start()
    for copy in copies:
        copy.wait()


def to_other_core(value, seq, step):
    pairs = [(2 * chip + core, 2 * (chip ^ step) + 1 - core) for chip in range(seq) for core in range(2)]
    return lax.ppermute(value, ("seq", "exp"), pairs)


def shards(seq, tokens, upstream, slot_params, slot_outputs, slot_input_grads):
    patches, half = tokens.shape
    n_slots = slot_params.shape[0] * seq
    extra = -(-6 * (n_slots // 8 + 1) // 128) * 128
    sds = jax.ShapeDtypeStruct
    cores = [(0, 1), (1, 0)]

    tokens_far, far = (lax.ppermute(x, "exp", cores) for x in (tokens, upstream))
    seed = call(seed_kernel, sds((8, 128), F32), "seed", seq, cost_estimate=LONG)()
    fours = seq // 4
    rows = (8, half + half // 2)
    chunks = call(pack_kernel, sds((1 if fours == 2 else seq, *rows), BF16), "pack", seq)(
        seed, slot_params, slot_outputs, slot_input_grads
    )
    if fours == 2:
        taken = to_other_core(chunks, seq, 4)
        pieces = [call(pair_kernel, sds((2, *rows), BF16), "pair", seq)(chunks, taken)]
        pieces += [to_other_core(pieces[0], seq, step) for step in range(1, 4)]
        slots = call(order_kernel, sds((seq, *rows), BF16), "order", seq)(*pieces)
    else:
        slots = lax.all_to_all(chunks, "seq", split_axis=0, concat_axis=0, tiled=True)
    other = lax.ppermute(slots, "exp", cores)
    by_slot = sds((n_slots, patches), F32)
    turned = sds((half, patches), BF16)
    near = call(near_kernel, (turned,) * 4 + (by_slot,) * 3, "near", seq, cost_estimate=LONG)(
        slots, tokens, tokens_far, upstream, far
    )
    chunk = (8, 2 * half + extra)
    cuts = [2 if fours == 2 and step != 3 else 1 for step in range(4)]
    *sends, col, row, disp = call(
        local_kernel,
        tuple(sds((fours // cut, *chunk), BF16) for cut in cuts for _ in range(cut)) + (by_slot,) * 3,
        "local",
        seq,
        [pltpu.VMEM((seq, 8, patches), F32)] * 2
        + [pltpu.VMEM((seq, 8, extra), F32)]
        + [pltpu.VMEM((3, seq, 8, patches), F32)] * 2,
    )(other, tokens, tokens_far, upstream, far, *near)
    first = [sends[sum(cuts[:step])] for step in range(4)]
    last = [sends[sum(cuts[: step + 1]) - 1] for step in range(4)]
    theirs = {step: to_other_core(last[step], seq, step) for step in (3, 2, 1)}
    ours = {step: to_other_core(first[step], seq, step) for step in (3, 2, 1) if cuts[step] == 2}
    merged = call(
        functools.partial(merge_kernel, groups=n_slots // 8 + 1, half=half),
        sds((1 if fours == 2 else fours, *chunk), BF16),
        "merge",
        seq,
    )(last[0], *theirs.values())
    if fours == 2:
        got = [to_other_core(merged, seq, 4), *({**theirs, **ours}[step] for step in (3, 2, 1))]
    else:
        same = [[4 * four + step for four in range(fours)] for step in range(4)]
        got = [lax.all_to_all(merged, "seq", split_axis=0, concat_axis=0, tiled=True, axis_index_groups=same)]
    param_grads, token_grads, slot_output_grads = call(
        finish_kernel,
        (sds((4, half), F32), sds((patches, half), BF16), sds((2, 2 * half), F32)),
        "finish",
        seq,
        [
            pltpu.VMEM((2, 8 * seq, patches), F32),
            pltpu.VMEM((4, half), F32),
            pltpu.VMEM((patches, half), BF16),
            pltpu.VMEM((2, 2 * half), F32),
            pltpu.SemaphoreType.DMA((4,)),
        ],
        out_specs=[pl.BlockSpec(memory_space=pl.ANY)] * 3,
    )(slots, other, col, row, disp, first[0], *got)
    return token_grads, param_grads, slot_output_grads


def solution(mesh):
    in_specs = (
        P(("group", "seq"), "exp"),
        P(("group", "seq"), "exp"),
        P(("group", "seq"), "exp"),
        P(("group", "seq", "exp"), None),
        P(("group", "seq", "exp"), None),
    )
    out_specs = (
        P(("group", "seq"), "exp"),
        P(("group", "seq"), "exp"),
        P(("group", "seq", "exp"), None),
    )
    return jax.shard_map(
        functools.partial(shards, mesh.shape["seq"]),
        mesh=mesh,
        in_specs=in_specs,
        out_specs=out_specs,
        check_vma=False,
    )
```
